32 devices in a mesh: group: 4 (over y, x), head: 8 (over z, core).
Axes of the slice: x: 2, y: 2, z: 4, core: 2. Of those that a mesh axis runs over, the one named last changes fastest.
Arguments:
- hidden: bfloat16 [2048, 8192], P(('group', 'head')), may hold values from -6 to 6
- norm_gain: bfloat16 [8192], replicated, may hold values from 0.25 to 1.75
- k_weight: bfloat16 [8192, 8192], P(None, 'head'), may hold values from -0.0625 to 0.0625
- k_bias: bfloat16 [8192], P('head'), may hold values from -3 to 3
- v_weight: bfloat16 [8192, 8192], P(None, 'head'), may hold values from -0.0625 to 0.0625
- v_bias: bfloat16 [8192], P('head'), may hold values from -3 to 3
- positions: int32 [2048], replicated, may hold values from 0 to 5119, as said below
- lengths: int32 [16], replicated, may hold values from 1 to 1021, as said below
- owner: int32 [16], replicated, may hold values from 0 to 3, as said below
Outputs:
- key_cache: bfloat16 [4096, 8192], P('group', 'head')
- value_cache: bfloat16 [4096, 8192], P('group', 'head')
The draws below stay inside these ranges and needn't reach their ends.
Inputs may be any that keep to these rules, and one draw needn't show every extreme that they name: lengths sum to 2048; the requests of one group hold at most 1024 tokens together, and one group holds exactly 1024. `owner`: every group owns exactly 4 requests. `positions`: positions rise by one from token to token inside a request.
All inputs are finite; a program needn't handle non-finite values.
Results may differ from the reference program's by a relative error of at most 0.0056.
Values may be sent and summed in bfloat16 or wider, within the bound.
No kernel may reach another device: no remote copies, remote signals or barrier semaphores. Data moves between devices by JAX's collectives and lax.ppermute only.
A program may use at most 128 MiB of HBM per device.

```python
import jax
import jax.numpy as jnp
from jax import lax

D = 8192
HD = 128
REQ_GROUP = 4
KVW = 8192
TOTAL = 2048
REQS = 16
N_GROUP = 4


def common_requests(key):
    key_heavy = jax.random.fold_in(key, 101)
    key_load = jax.random.fold_in(key, 102)
    key_owner = jax.random.fold_in(key, 103)
    key_split = jax.random.fold_in(key, 104)
    key_prefix = jax.random.fold_in(key, 105)
    cap = TOTAL // 2
    rest = TOTAL - cap
    others = N_GROUP - 1
    base = rest // others
    jitter = jax.random.randint(key_load, (others,), -(base // 4), base // 4 + 1).astype(jnp.int32)
    jitter = jnp.where(jnp.arange(others) == others - 1, 0, jitter).astype(jnp.int32)
    light = base + jitter
    light = light.at[others - 1].set(rest - jnp.sum(light[:others - 1])).astype(jnp.int32)
    order = jax.random.permutation(key_heavy, N_GROUP).astype(jnp.int32)
    ranked = jnp.concatenate([jnp.array([cap], jnp.int32), light]).astype(jnp.int32)
    loads = jnp.zeros((N_GROUP,), jnp.int32).at[order].set(ranked)
    part = loads // REQ_GROUP
    cut = jax.random.randint(key_split, (N_GROUP, REQ_GROUP), 0, 1 << 20).astype(jnp.int32) % (part[:, None] // 2 + 1)
    pieces = part[:, None] - cut
    last = loads - jnp.sum(pieces[:, :REQ_GROUP - 1], axis=1)
    pieces = pieces.at[:, REQ_GROUP - 1].set(last).astype(jnp.int32)
    heavy_row = jnp.concatenate([jnp.array([cap - REQ_GROUP + 1], jnp.int32), jnp.ones((REQ_GROUP - 1,), jnp.int32)]).astype(jnp.int32)
    is_heavy = jnp.arange(N_GROUP, dtype=jnp.int32)[:, None] == order[0]
    pieces = jnp.where(is_heavy, heavy_row[None, :], pieces).astype(jnp.int32)
    owner = jax.random.permutation(key_owner, jnp.repeat(jnp.arange(N_GROUP, dtype=jnp.int32), REQ_GROUP)).astype(jnp.int32)
    same = owner[:, None] == owner[None, :]
    before = jnp.arange(REQS)[None, :] < jnp.arange(REQS)[:, None]
    rank = jnp.sum(same & before, axis=1).astype(jnp.int32)
    lengths = pieces[owner, rank].astype(jnp.int32)
    ends = jnp.cumsum(lengths).astype(jnp.int32)
    token = jnp.arange(TOTAL, dtype=jnp.int32)
    request = jnp.sum(ends[None, :] <= token[:, None], axis=1).astype(jnp.int32)
    starts = (ends - lengths).astype(jnp.int32)
    prefix = jax.random.randint(key_prefix, (REQS,), 0, 4096).astype(jnp.int32)
    prefix = prefix.at[0].set(4096 + cap - lengths[0]).astype(jnp.int32)
    prefix = prefix.at[1].set(0).astype(jnp.int32)
    positions = (prefix[request] + token - starts[request]).astype(jnp.int32)
    return (lengths, owner, positions)


def draw_lengths(key, part):
    lengths, owner, positions = common_requests(key)
    return lengths


def draw_owner(key, part):
    lengths, owner, positions = common_requests(key)
    return owner


def draw_positions(key, part):
    lengths, owner, positions = common_requests(key)
    return positions


def levels(stream_key, extent, cuts, smallest, largest):
    level, own = 1.0, jax.random.fold_in(stream_key, 6)
    for axis_at, blocks in cuts:
        heights = jnp.exp(jax.random.uniform(jax.random.fold_in(own, axis_at), (blocks,), jnp.float32, smallest / len(cuts), largest / len(cuts)))
        level = level * jnp.repeat(heights, extent[axis_at] // blocks).reshape([-1 if axis == axis_at else 1 for axis in range(len(extent))])
    return level


def normal_values(own_key, shape, width, limit, shards=(), kind=jnp.bfloat16):
    drawn = jax.random.normal(own_key, shape, jnp.float32) * width
    if len(shards) > 0:
        drawn = levels(own_key, shape, shards, -0.22, 0.18) * drawn
    return jnp.clip(drawn, min=-limit, max=limit).astype(kind)


def setup_inputs(seed: int = 0) -> dict:
    key_list = jax.random.split(jax.random.key(seed), 10)
    return {
        "hidden": normal_values(key_list[0], (TOTAL, D), 1.0, 6.0, ((0, 32),)),
        "norm_gain": jnp.clip(1.0 + 0.15 * jax.random.normal(key_list[1], (D,), jnp.float32), 0.25, 1.75).astype(jnp.bfloat16),
        "k_weight": normal_values(key_list[2], (D, KVW), D ** -0.5, 0.0625, ((1, 8),)),
        "k_bias": normal_values(key_list[3], (KVW,), 0.5, 3.0, ((0, 8),)),
        "v_weight": normal_values(key_list[4], (D, KVW), D ** -0.5, 0.0625, ((1, 8),)),
        "v_bias": normal_values(key_list[5], (KVW,), 0.5, 3.0, ((0, 8),)),
        "positions": draw_positions(jax.random.fold_in(key_list[9], 71), 0),
        "lengths": draw_lengths(jax.random.fold_in(key_list[9], 71), 0),
        "owner": draw_owner(jax.random.fold_in(key_list[9], 71), 0),
    }


def rotate(raw, pos):
    count = raw.shape[0]
    half = HD // 2
    x = raw.astype(jnp.float32).reshape(count, -1, HD)
    freq = jnp.exp(jnp.arange(half, dtype=jnp.float32) * (-2.0 / HD * jnp.log(jnp.float32(1000000.0))))
    angle = pos.astype(jnp.float32)[:, None] * freq[None, :]
    cosine = jnp.cos(angle)[:, None, :]
    sine = jnp.sin(angle)[:, None, :]
    first = x[:, :, :half]
    second = x[:, :, half:]
    out = jnp.concatenate([first * cosine - second * sine, second * cosine + first * sine], axis=2)
    return out.reshape(count, -1).astype(jnp.bfloat16)

def cache_map(lengths, owner, group, cap):
    inside = owner == group
    own_len = jnp.where(inside, lengths, 0).astype(jnp.int32)
    start = (jnp.cumsum(lengths) - lengths).astype(jnp.int32)
    local = (jnp.cumsum(own_len) - own_len).astype(jnp.int32)
    row = jnp.arange(cap, dtype=jnp.int32)[:, None]
    match = inside[None, :] & (row >= local[None, :]) & (row < (local + lengths)[None, :])
    source = lax.optimization_barrier(jnp.sum(jnp.where(match, start[None, :] + row - local[None, :], 0), axis=1)).astype(jnp.int32)
    return (source, jnp.any(match, axis=1))

def reference(hidden, norm_gain, k_weight, k_bias, v_weight, v_bias, positions, lengths, owner):
    rows = hidden.astype(jnp.float32)
    scale = lax.rsqrt(lax.optimization_barrier(jnp.mean(rows * rows, axis=1, keepdims=True)) + 1e-06)
    normed = (rows * scale * norm_gain.astype(jnp.float32)).astype(jnp.bfloat16)
    key_raw = (jnp.dot(normed, k_weight, preferred_element_type=jnp.float32) + k_bias.astype(jnp.float32)).astype(jnp.bfloat16)
    values = (jnp.dot(normed, v_weight, preferred_element_type=jnp.float32) + v_bias.astype(jnp.float32)).astype(jnp.bfloat16)
    keys = rotate(key_raw, positions)
    cap = TOTAL // 2
    key_parts = []
    value_parts = []
    for group in range(N_GROUP):
        source, valid = cache_map(lengths, owner, group, cap)
        zero = jnp.zeros((), jnp.bfloat16)
        key_parts.append(jnp.where(valid[:, None], jnp.take(keys, source, axis=0), zero))
        value_parts.append(jnp.where(valid[:, None], jnp.take(values, source, axis=0), zero))
    return (jnp.concatenate(key_parts, axis=0), jnp.concatenate(value_parts, axis=0))
```

```python
import functools

import jax
import jax.numpy as jnp
from jax import lax
from jax.experimental import pallas as pl
from jax.experimental.pallas import tpu as pltpu
from jax.sharding import PartitionSpec as P

HD = 128
BF = jnp.bfloat16
F32 = jnp.float32
MIB = 1 << 20
VMEM = pltpu.VMEM
ANY = pl.ANY


def rotate(raw, pos):
    count = raw.shape[0]
    half = HD // 2
    x = raw.astype(jnp.float32).reshape(count, -1, HD)
    freq = jnp.exp(
        jnp.arange(half, dtype=jnp.float32) * (-2.0 / HD * jnp.log(jnp.float32(1000000.0)))
    )
    angle = pos.astype(jnp.float32)[:, None] * freq[None, :]
    cosine = jnp.cos(angle)[:, None, :]
    sine = jnp.sin(angle)[:, None, :]
    first = x[:, :, :half]
    second = x[:, :, half:]
    out = jnp.concatenate([first * cosine - second * sine, second * cosine + first * sine], axis=2)
    return out.reshape(count, -1).astype(jnp.bfloat16)


def cache_map(lengths, owner, group, cap):
    inside = owner == group
    own_len = jnp.where(inside, lengths, 0)
    start = jnp.cumsum(lengths) - lengths
    local = jnp.cumsum(own_len) - own_len
    row = jnp.arange(cap, dtype=jnp.int32)[:, None]
    match = inside[None, :] & (row >= local[None, :]) & (row < (local + lengths)[None, :])
    source = jnp.sum(jnp.where(match, start[None, :] + row - local[None, :], 0), axis=1)
    return (source, jnp.any(match, axis=1))


def gathered(hidden, norm_gain, k_weight, k_bias, v_weight, v_bias, positions, lengths, owner):
    rows = hidden.astype(jnp.float32)
    scale = lax.rsqrt(jnp.mean(rows * rows, axis=1, keepdims=True) + 1e-06)
    normed = (rows * scale * norm_gain.astype(jnp.float32)).astype(jnp.bfloat16)
    group_index = lax.axis_index("group")
    head_count = lax.axis_size("head")
    rows_dev = hidden.shape[0]
    width = k_weight.shape[1]
    cap = rows_dev * lax.axis_size("group") * head_count // 2
    piece = lax.all_gather(normed, "head", axis=0, tiled=True)
    key_raw = (
        jnp.dot(piece, k_weight, preferred_element_type=jnp.float32) + k_bias.astype(jnp.float32)
    ).astype(jnp.bfloat16)
    values = (
        jnp.dot(piece, v_weight, preferred_element_type=jnp.float32) + v_bias.astype(jnp.float32)
    ).astype(jnp.bfloat16)
    projected = jnp.concatenate([key_raw, values], axis=1)
    source, valid = cache_map(lengths, owner, group_index, cap)
    zero = jnp.zeros((), jnp.bfloat16)
    everything = lax.all_gather(projected, "group", axis=0, tiled=True)
    cache = jnp.where(valid[:, None], jnp.take(everything, source, axis=0), zero)
    key_cache = cache[:, :width]
    value_cache = cache[:, width:]
    row_pos = jnp.take(positions, source, axis=0)
    key_cache = jnp.where(valid[:, None], rotate(key_cache, row_pos), zero)
    return (key_cache, value_cache)


def norm_kernel(x_ref, gain_ref, lo_ref, hi_ref):
    half = lo_ref.shape[0]
    step = 16
    for at in range(0, x_ref.shape[0], step):
        x = x_ref[at : at + step, :].astype(F32)
        scale = lax.rsqrt(jnp.mean(x * x, axis=1, keepdims=True) + 1e-06)
        y = (x * scale * gain_ref[...].astype(F32)).astype(BF)
        if at < half:
            lo_ref[at : at + step, :] = y
        else:
            hi_ref[at - half : at - half + step, :] = y


def normalise(hidden, gain):
    rows, wide = hidden.shape
    half = jax.ShapeDtypeStruct((rows // 2, wide), BF)
    return pl.pallas_call(
        norm_kernel,
        out_shape=(half, half),
        name="norm",
        cost_estimate=pl.CostEstimate(flops=5 * rows * wide, bytes_accessed=4 * rows * wide, transcendentals=rows),
        compiler_params=pltpu.CompilerParams(vmem_limit_bytes=16 * MIB),
    )(hidden, gain.reshape(1, wide))


def project(parts, m, x_ref, wk, wv, kb, vb, cos, sin, outs, before):
    width = wk.shape[1]
    tile = 256
    split = outs[0].shape[0]

    def put(at, y):
        outs[0][:, pl.ds(at, tile)] = y[:split]
        outs[1][:, pl.ds(at, tile)] = y[split:]

    def keys(i, carry):
        at = pl.multiple_of(i * tile, tile)
        raw = jnp.dot(x_ref[...], wk[:, pl.ds(at, tile)], preferred_element_type=F32)
        raw = (raw + kb[:, pl.ds(at, tile)].astype(F32)).astype(BF).astype(F32)
        c = jnp.concatenate([cos[pl.ds(pl.multiple_of(o, 8), n), :] for o, n in parts], axis=0)
        s = jnp.concatenate([sin[pl.ds(pl.multiple_of(o, 8), n), :] for o, n in parts], axis=0)
        heads = []
        for h in range(tile // HD):
            one = raw[:, h * HD : (h + 1) * HD]
            heads.append(one * c + pltpu.roll(one, HD // 2, axis=1) * s)
        put(at, jnp.concatenate(heads, axis=1).astype(BF))
        return carry

    def values(i, carry):
        at = pl.multiple_of(i * tile, tile)
        raw = jnp.dot(x_ref[...], wv[:, pl.ds(at, tile)], preferred_element_type=F32)
        put(pl.multiple_of(width + i * tile, tile), (raw + vb[:, pl.ds(at, tile)].astype(F32)).astype(BF))
        return carry

    if before is None:
        lax.fori_loop(0, width // tile, keys, 0)
        lax.fori_loop(0, width // tile, values, 0)
    else:
        for i in range(width // tile):
            before(0, i)
            keys(i, 0)
        for i in range(width // tile):
            before(1, i)
            values(i, 0)


def part_offsets(layout):
    head = lax.axis_index("head")
    chip, core = head // 2, head % 2
    out = []
    for w, j, u, n in layout:
        out.append(((chip ^ w) * 128 + (core ^ j) * 64 + u * 32, n))
    return out


def first_kernel(layout, lo, hi, slo, shi, wk, wv, kb, vb, cos, sin, p0, p1, wko, wvo, x, xsem, wsem):
    width = wk.shape[1]
    tile = 256
    half = lo.shape[0]
    loads = []
    for i, src in enumerate((lo, hi, slo, shi)):
        loads.append(pltpu.make_async_copy(src, x.at[pl.ds(i * half, half)], xsem.at[i]))
        loads[-1].start()
    copies = []
    for a, (src, dst) in enumerate(((wk, wko), (wv, wvo))):
        for i in range(width // tile):
            cols = pl.ds(i * tile, tile)
            copies.append(pltpu.make_async_copy(src.at[:, cols], dst.at[:, cols], wsem.at[a * (width // tile) + i]))
            copies[-1].start()
    for one in loads:
        one.wait()

    def before(a, i):
        copies[a * (width // tile) + i].wait()

    project(part_offsets(layout), x.shape[0], x, wko, wvo, kb, vb, cos, sin, (p0, p1), before)


def wave_kernel(layout, ends, *refs):
    count = len(layout)
    sources = refs[: count * (2 if ends else 1)]
    wk, wv, kb, vb, cos, sin, p0, p1, x, sem = refs[len(sources) :]
    row = 0
    copies = []
    chip = lax.axis_index("head") // 2
    at_end = (chip == 0) | (chip == 3)
    for i, (w, j, u, n) in enumerate(layout):
        dst = x.at[pl.ds(row, n)]
        if ends:
            pl.when(jnp.logical_not(at_end))(pltpu.make_async_copy(sources[i], dst, sem.at[i]).start)
            pl.when(at_end)(pltpu.make_async_copy(sources[count + i], dst, sem.at[i]).start)
        else:
            pltpu.make_async_copy(sources[i], dst, sem.at[i]).start()
        copies.append(pltpu.make_async_copy(sources[i], dst, sem.at[i]))
        row += n
    for one in copies:
        one.wait()
    project(part_offsets(layout), x.shape[0], x, wk, wv, kb, vb, cos, sin, (p0, p1), None)


def cost(m, deep, width, weights):
    return pl.CostEstimate(
        flops=2 * m * deep * width * 2,
        bytes_accessed=2 * (m * deep + m * width * 2 + (deep * width * 2 if weights else 0)),
        transcendentals=0,
    )


def first_wave(layout, own, sibling, wk, wv, rest):
    deep, width = wk.shape
    m = sum(n for _, _, _, n in layout)
    half = jax.ShapeDtypeStruct((m // 2, 2 * width), BF)
    kept = VMEM((deep, width), BF)
    full = pl.BlockSpec(memory_space=VMEM)
    hbm = pl.BlockSpec(memory_space=ANY)
    return pl.pallas_call(
        functools.partial(first_kernel, layout),
        out_shape=(half, half, kept, kept),
        in_specs=[hbm] * 6 + [full] * 4,
        out_specs=(full,) * 4,
        scratch_shapes=[VMEM((m, deep), BF), pltpu.SemaphoreType.DMA((4,)), pltpu.SemaphoreType.DMA((2 * width // 256,))],
        name="wave0",
        cost_estimate=cost(m, deep, width, True),
        compiler_params=pltpu.CompilerParams(vmem_limit_bytes=16 * MIB),
    )(*own, *sibling, wk, wv, *rest)


def wave(name, layout, sources, ends, wk, wv, rest):
    deep, width = wk.shape
    m = sum(n for _, _, _, n in layout)
    half = jax.ShapeDtypeStruct((m // 2, 2 * width), BF)
    full = pl.BlockSpec(memory_space=VMEM)
    hbm = pl.BlockSpec(memory_space=ANY)
    return pl.pallas_call(
        functools.partial(wave_kernel, layout, ends),
        out_shape=(half, half),
        in_specs=[hbm] * len(sources) + [full] * 6,
        out_specs=(full, full),
        scratch_shapes=[VMEM((m, deep), BF), pltpu.SemaphoreType.DMA((len(layout),))],
        name=name,
        cost_estimate=cost(m, deep, width, False),
        compiler_params=pltpu.CompilerParams(vmem_limit_bytes=16 * MIB),
    )(*sources, wk, wv, *rest)


def place_kernel(units, lengths, owner, *refs):
    arrays = max(unit[4] for unit in units) + 1
    sources = refs[:arrays]
    key_out, value_out, rows, sem = refs[arrays:]
    width = key_out.shape[1]
    group = lax.axis_index("group")
    head = lax.axis_index("head")
    copies = []
    for i, (d, w, j, u, a, row, n) in enumerate(units):
        at = (group ^ d) * 512 + ((head // 2) ^ w) * 128 + ((head % 2) ^ j) * 64 + u * 32
        copy = pltpu.make_async_copy(
            sources[a].at[pl.ds(row, n)], rows.at[pl.ds(pl.multiple_of(at, 32), n)], sem.at[i]
        )
        copy.start()
        copies.append(copy)
    key_out[...] = jnp.zeros_like(key_out)
    value_out[...] = jnp.zeros_like(value_out)
    for copy in copies:
        copy.wait()
    tile, window = 128, 256
    total = rows.shape[0]

    def request(q, carry):
        start, local = carry
        length = lengths[q]
        mine = owner[q] == group

        @pl.when(mine)
        def _():
            def step(t, c):
                top = pl.multiple_of(t * tile, tile)
                base = start + top - local
                at = pl.multiple_of(jnp.clip((base >> 4) << 4, 0, total - window), 16)
                src = at + lax.broadcasted_iota(jnp.int32, (tile, window), 1)
                dst = base + lax.broadcasted_iota(jnp.int32, (tile, window), 0)
                hit = (src == dst) & (src >= start) & (src < start + length)
                pick = jnp.where(hit, 1.0, 0.0).astype(BF)
                for part, out in ((0, key_out), (1, value_out)):
                    moved = jnp.dot(pick, rows[pl.ds(at, window), part * width : (part + 1) * width], preferred_element_type=F32)
                    out[pl.ds(top, tile), :] += moved.astype(BF)
                return c

            lax.fori_loop(local // tile, (local + length - 1) // tile + 1, step, 0)

        return (start + length, local + jnp.where(mine, length, 0))

    lax.fori_loop(0, lengths.shape[0], request, (jnp.int32(0), jnp.int32(0)))


def place(units, arrays, lengths, owner, cap, width, total):
    out = jax.ShapeDtypeStruct((cap, width), BF)
    smem = pl.BlockSpec(memory_space=pltpu.SMEM)
    hbm = pl.BlockSpec(memory_space=ANY)
    full = pl.BlockSpec(memory_space=VMEM)
    return pl.pallas_call(
        functools.partial(place_kernel, units),
        out_shape=(out, out),
        in_specs=[smem, smem] + [hbm] * len(arrays),
        out_specs=(full, full),
        scratch_shapes=[VMEM((total, 2 * width), BF), pltpu.SemaphoreType.DMA((len(units),))],
        name="place",
        cost_estimate=pl.CostEstimate(flops=0, bytes_accessed=20 * MIB, transcendentals=0),
        compiler_params=pltpu.CompilerParams(vmem_limit_bytes=28 * MIB),
    )(lengths, owner, *arrays)


def pipelined(hidden, norm_gain, k_weight, k_bias, v_weight, v_bias, positions, lengths, owner):
    width = k_weight.shape[1]
    group = lax.axis_index("group")

    def line(x, pairs):
        return lax.ppermute(x, "head", [(2 * a + c, 2 * b + c) for a, b in pairs for c in range(2)])

    def sibling(x):
        return lax.ppermute(x, "head", [(i, i ^ 1) for i in range(8)])

    def across(x, bit):
        return lax.ppermute(x, "group", [(i, i ^ bit) for i in range(4)])

    own = normalise(hidden, norm_gain)
    far = [line(x, [(0, 2), (1, 3), (2, 0), (3, 1)]) for x in own]
    near = [line(x, [(0, 1), (1, 0), (2, 3), (3, 2)]) for x in own]
    middle = [line(x, [(1, 2), (2, 1), (0, 0), (3, 3)]) for x in own]
    relay = [line(x, [(1, 0), (2, 3), (0, 1), (3, 2)]) for x in far]
    own_s, far_s, near_s, middle_s, relay_s = (
        [sibling(x) for x in xs] for xs in (own, far, near, middle, relay)
    )

    half = HD // 2
    freq = jnp.exp(jnp.arange(half, dtype=F32) * (-2.0 / HD * jnp.log(F32(1000000.0))))
    pos = lax.dynamic_slice(positions, (group * 512,), (512,)).astype(F32)
    angle = pos[:, None] * freq[None, :]
    cosine, sine = jnp.cos(angle), jnp.sin(angle)
    cos = jnp.concatenate([cosine, cosine], axis=1)
    sin = jnp.concatenate([-sine, sine], axis=1)
    rest = (k_bias.reshape(1, width), v_bias.reshape(1, width), cos, sin)

    units, arrays = [], []

    def spread(layouts, parts):
        got = [parts, [across(p, 1) for p in parts], [across(p, 2) for p in parts]]
        got.append([across(got[1][0], 2), across(got[2][1], 1)])
        for d, pair in enumerate(got):
            for layout, array in zip(layouts, pair):
                row = 0
                for w, j, u, n in layout:
                    units.append((d, w, j, u, len(arrays), row, n))
                    row += n
                arrays.append(array)

    layout = [(0, 0, 0, 32), (0, 0, 1, 32), (0, 1, 0, 32), (0, 1, 1, 32)]
    p0, p1, wk, wv = first_wave(layout, own, own_s, k_weight, v_weight, rest)
    spread([layout[:2], layout[2:]], [p0, p1])
    for u in range(2):
        layout = [(2, 0, u, 32), (2, 1, u, 32), (1, 0, u, 32), (1, 1, u, 32)]
        sources = [far[u], far_s[u], near[u], near_s[u]]
        parts = wave("wave%d" % (1 + u), layout, sources, False, wk, wv, rest)
        spread([layout[:2], layout[2:]], parts)
    for u in range(2):
        layout = [(3, 0, u, 32), (3, 1, u, 32)]
        sources = [middle[u], middle_s[u], relay[u], relay_s[u]]
        parts = wave("wave%d" % (3 + u), layout, sources, True, wk, wv, rest)
        spread([layout[:1], layout[1:]], parts)
    return place(units, arrays, lengths, owner, 1024, width, 2048)


def solution(mesh):
    in_specs = (
        P(("group", "head"), None),
        P(),
        P(None, "head"),
        P("head"),
        P(None, "head"),
        P("head"),
        P(),
        P(),
        P(),
    )
    out_specs = (P("group", "head"), P("group", "head"))
    square = mesh.shape["group"] == 4 and mesh.shape["head"] == 8
    return jax.shard_map(
        pipelined if square else gathered, mesh=mesh, in_specs=in_specs, out_specs=out_specs, check_vma=False
    )
```

```python
import functools

import jax
import jax.numpy as jnp
from jax import lax
from jax.experimental import pallas as pl
from jax.experimental.pallas import tpu as pltpu
from jax.sharding import PartitionSpec as P

HD = 128
BF = jnp.bfloat16
F32 = jnp.float32
MIB = 1 << 20
VMEM = pltpu.VMEM
ANY = pltpu.HBM


def rotate(raw, pos):
    count = raw.shape[0]
    half = HD // 2
    x = raw.astype(jnp.float32).reshape(count, -1, HD)
    freq = jnp.exp(
        jnp.arange(half, dtype=jnp.float32) * (-2.0 / HD * jnp.log(jnp.float32(1000000.0)))
    )
    angle = pos.astype(jnp.float32)[:, None] * freq[None, :]
    cosine = jnp.cos(angle)[:, None, :]
    sine = jnp.sin(angle)[:, None, :]
    first = x[:, :, :half]
    second = x[:, :, half:]
    out = jnp.concatenate([first * cosine - second * sine, second * cosine + first * sine], axis=2)
    return out.reshape(count, -1).astype(jnp.bfloat16)


def cache_map(lengths, owner, group, cap):
    inside = owner == group
    own_len = jnp.where(inside, lengths, 0)
    start = jnp.cumsum(lengths) - lengths
    local = jnp.cumsum(own_len) - own_len
    row = jnp.arange(cap, dtype=jnp.int32)[:, None]
    match = inside[None, :] & (row >= local[None, :]) & (row < (local + lengths)[None, :])
    source = jnp.sum(jnp.where(match, start[None, :] + row - local[None, :], 0), axis=1)
    return (source, jnp.any(match, axis=1))


def gathered(hidden, norm_gain, k_weight, k_bias, v_weight, v_bias, positions, lengths, owner):
    rows = hidden.astype(jnp.float32)
    scale = lax.rsqrt(jnp.mean(rows * rows, axis=1, keepdims=True) + 1e-06)
    normed = (rows * scale * norm_gain.astype(jnp.float32)).astype(jnp.bfloat16)
    group_index = lax.axis_index("group")
    head_count = lax.axis_size("head")
    rows_dev = hidden.shape[0]
    width = k_weight.shape[1]
    cap = rows_dev * lax.axis_size("group") * head_count // 2
    piece = lax.all_gather(normed, "head", axis=0, tiled=True)
    key_raw = (
        jnp.dot(piece, k_weight, preferred_element_type=jnp.float32) + k_bias.astype(jnp.float32)
    ).astype(jnp.bfloat16)
    values = (
        jnp.dot(piece, v_weight, preferred_element_type=jnp.float32) + v_bias.astype(jnp.float32)
    ).astype(jnp.bfloat16)
    projected = jnp.concatenate([key_raw, values], axis=1)
    source, valid = cache_map(lengths, owner, group_index, cap)
    zero = jnp.zeros((), jnp.bfloat16)
    everything = lax.all_gather(projected, "group", axis=0, tiled=True)
    cache = jnp.where(valid[:, None], jnp.take(everything, source, axis=0), zero)
    key_cache = cache[:, :width]
    value_cache = cache[:, width:]
    row_pos = jnp.take(positions, source, axis=0)
    key_cache = jnp.where(valid[:, None], rotate(key_cache, row_pos), zero)
    return (key_cache, value_cache)


def norm_kernel(x_ref, gain_ref, out_ref, lo_ref, hi_ref):
    step = 16
    first = lo_ref.shape[0]
    gain = gain_ref[...].astype(F32)
    for at in range(0, x_ref.shape[0], step):
        x = x_ref[at : at + step, :].astype(F32)
        scale = lax.rsqrt(jnp.mean(x * x, axis=1, keepdims=True) + 1e-06)
        y = (x * scale * gain).astype(BF)
        out_ref[at : at + step, :] = y
        if at < first:
            lo_ref[at : at + step, :] = y
        else:
            hi_ref[at - first : at - first + step, :] = y


def normalise(hidden, gain):
    rows, wide = hidden.shape
    return pl.pallas_call(
        norm_kernel,
        out_shape=tuple(VMEM((n, wide), BF) for n in (rows, *PART)),
        name="norm",
        cost_estimate=pl.CostEstimate(flops=rows * wide, bytes_accessed=rows, transcendentals=rows),
        compiler_params=pltpu.CompilerParams(vmem_limit_bytes=16 * MIB),
    )(hidden, gain.reshape(1, wide))


PART = (32, 32)
PART_AT = (0, 64)


def piece_at(step, part):
    return pl.multiple_of(((lax.axis_index("head") // 2) ^ step) * 128 + PART_AT[part], 32)


def rotation(pieces, cos, sin):
    return [
        jnp.concatenate([table[pl.ds(piece_at(*piece), 2 * PART[piece[1]]), :] for piece in pieces], axis=0)
        for table in (cos, sin)
    ]


def load_rows(x, pieces, sources, sem, start=True, wait=True):
    core = lax.axis_index("head") % 2
    base = 0
    for i, ((step, part), (own, sib, row)) in enumerate(zip(pieces, sources)):
        n = PART[part]
        for j, src in enumerate((own, sib)):
            at = pl.multiple_of(base + (core ^ j) * n, 16)
            copy = pltpu.make_async_copy(src.at[pl.ds(row, n)], x.at[pl.ds(at, n)], sem.at[2 * i + j])
            if start:
                copy.start()
            if wait:
                copy.wait()
        base += 2 * n


def turn(raw, c, s):
    raw = raw.astype(BF).astype(F32)
    heads = []
    for h in range(raw.shape[1] // HD):
        one = raw[:, h * HD : (h + 1) * HD]
        heads.append(one * c + pltpu.roll(one, HD // 2, axis=1) * s)
    return jnp.concatenate(heads, axis=1).astype(BF)


WHOLE = [(0, 0), (0, 1)]


def both(own, sib):
    return [(own, sib, 0), (own, sib, PART[0])]


def wave_kernel(pieces, kind, count, *refs):
    sources = refs[:count]
    wk, wv, kb, vb, cos, sin = refs[count : count + 6]
    outs, x, blocks, sem, wsem = refs[count + 6 : -4], *refs[-4:]
    deep, width = wk.shape
    depth, _, tile = blocks.shape
    each = width // tile
    half = deep // 2
    copies = []
    for i in range(2 * each):
        cols = pl.ds(i % each * tile, tile)
        copies.append(
            [
                pltpu.make_async_copy(
                    (wk, wv)[i // each].at[pl.ds(j * half, half), cols],
                    blocks.at[i % depth, pl.ds(j * half, half)],
                    wsem.at[2 * i + j],
                )
                for j in range(2)
            ]
        )

    def fetch(i):
        for copy in copies[i]:
            copy.start()

    load = functools.partial(load_rows, x, pieces)
    if kind == "relayed":
        chip = lax.axis_index("head") // 2
        at_end = (chip == 0) | (chip == 3)
        rows = both(*sources[:2])
        ends = both(*sources[2:])
        pl.when(jnp.logical_not(at_end))(lambda: load(rows, sem, wait=False))
        pl.when(at_end)(lambda: load(ends, sem, wait=False))
    else:
        rows = both(*sources) if kind == "whole" else [(sources[i], sources[i + 1], 0) for i in range(0, count, 2)]
        load(rows, sem, wait=False)
    for i in range(depth):
        fetch(i)
    c, s = rotation(pieces, cos, sin)
    load(rows, sem, start=False)
    part = x.shape[0] // len(outs)
    for i in range(2 * each):
        for copy in copies[i]:
            copy.wait()
        raw = jnp.dot(x[...], blocks[i % depth], preferred_element_type=F32)
        if i < each:
            y = turn(raw + kb[:, i * tile : (i + 1) * tile].astype(F32), c, s)
        else:
            at = (i - each) * tile
            y = (raw + vb[:, at : at + tile].astype(F32)).astype(BF)
        for k, out in enumerate(outs):
            for j in range(out.shape[0] // part):
                out[j * part : (j + 1) * part, i * tile : (i + 1) * tile] = y[k * part : (k + 1) * part]
        if i + depth < 2 * each:
            fetch(i + depth)


def cost(m, deep, width, weights):
    return pl.CostEstimate(flops=m * width, bytes_accessed=2 * m * width, transcendentals=0)


def in_hbm(x):
    return pltpu.with_memory_space_constraint(x, pltpu.HBM)


def wave(name, pieces, kind, sources, wk, wv, rest, split=1, copies=1):
    deep, width = wk.shape
    m = sum(2 * PART[part] for _, part in pieces)
    tile, depth = 256, 3
    full = pl.BlockSpec(memory_space=VMEM)
    hbm = pl.BlockSpec(memory_space=ANY)
    return pl.pallas_call(
        functools.partial(wave_kernel, pieces, kind, len(sources)),
        out_shape=[VMEM((copies * m // split, 2 * width), BF)] * split,
        in_specs=[hbm] * (len(sources) + 2) + [full] * 4,
        out_specs=[full] * split,
        scratch_shapes=[
            VMEM((m, deep), BF),
            VMEM((depth, deep, tile), BF),
            pltpu.SemaphoreType.DMA((2 * len(pieces),)),
            pltpu.SemaphoreType.DMA((4 * width // tile,)),
        ],
        name=name,
        cost_estimate=cost(m, deep, width, True),
        compiler_params=pltpu.CompilerParams(vmem_limit_bytes=24 * MIB),
    )(*sources, wk, wv, *rest)


def place_kernel(units, lengths, owner, *refs):
    count = max(unit[3] for unit in units) + 1
    sources = refs[:count]
    key_out, value_out, rows = refs[count:]
    width = key_out.shape[1]
    group = lax.axis_index("group")
    chip = lax.axis_index("head") // 2
    for d, step, at, a, row, n in units:
        whose = d[0] if isinstance(d, tuple) else group ^ d
        to = pl.multiple_of(whose * 512 + (chip ^ step) * 128 + at, 16)
        rows[pl.ds(to, n), :] = sources[a][row : row + n, :]
    key_out[...] = jnp.zeros_like(key_out)
    value_out[...] = jnp.zeros_like(value_out)
    tile, window = 128, 256
    total = rows.shape[0]

    def request(q, carry):
        start, local = carry
        length = lengths[q]
        mine = owner[q] == group

        @pl.when(mine)
        def _():
            def step(t, c):
                top = pl.multiple_of(t * tile, tile)
                base = start + top - local
                at = pl.multiple_of(jnp.clip((base >> 7) << 7, 0, total - window), 128)
                lane = lax.broadcasted_iota(jnp.int32, (tile, window), 1)
                p = lane & 127
                first, second = PART
                stay = (p < first) | (p >= 128 - second)
                src = at + lane + jnp.where(stay, 0, jnp.where(p < 2 * first, second, -first))
                dst = base + lax.broadcasted_iota(jnp.int32, (tile, window), 0)
                hit = (src == dst) & (src >= start) & (src < start + length)
                pick = jnp.where(hit, 1.0, 0.0).astype(BF)
                for part, out in ((0, key_out), (1, value_out)):
                    moved = jnp.dot(pick, rows[pl.ds(at, window), part * width : (part + 1) * width], preferred_element_type=F32)
                    out[pl.ds(top, tile), :] += moved.astype(BF)
                return c

            lax.fori_loop(local // tile, (local + length - 1) // tile + 1, step, 0)

        return (start + length, local + jnp.where(mine, length, 0))

    lax.fori_loop(0, lengths.shape[0], request, (jnp.int32(0), jnp.int32(0)))


def place(units, arrays, lengths, owner, cap, width, total):
    out = jax.ShapeDtypeStruct((cap, width), BF)
    smem = pl.BlockSpec(memory_space=pltpu.SMEM)
    full = pl.BlockSpec(memory_space=VMEM)
    return pl.pallas_call(
        functools.partial(place_kernel, units),
        out_shape=(out, out),
        in_specs=[smem, smem] + [full] * len(arrays),
        out_specs=(full, full),
        scratch_shapes=[VMEM((total, 2 * width), BF)],
        name="place",
        cost_estimate=pl.CostEstimate(flops=0, bytes_accessed=20 * MIB, transcendentals=0),
        compiler_params=pltpu.CompilerParams(vmem_limit_bytes=28 * MIB),
    )(lengths, owner, *arrays)


def pipelined(hidden, norm_gain, k_weight, k_bias, v_weight, v_bias, positions, lengths, owner):
    width = k_weight.shape[1]
    group = lax.axis_index("group")

    def line(x, pairs):
        return lax.ppermute(x, "head", [(2 * a + c, 2 * b + c) for a, b in pairs for c in range(2)])

    def sibling(x):
        return lax.ppermute(x, "head", [(i, i ^ 1) for i in range(8)])

    def across(x, bit):
        return lax.ppermute(x, "group", [(i, i ^ bit) for i in range(4)])

    far_pairs = [(0, 2), (1, 3), (2, 0), (3, 1)]
    near_pairs = [(0, 1), (1, 0), (2, 3), (3, 2)]
    middle_pairs = [(1, 2), (2, 1)]

    def after(x, *done):
        return lax.optimization_barrier((x,) + done)[0]

    own, lo, hi = normalise(hidden, norm_gain)
    own_s = sibling(own)
    far1, near1 = line(lo, far_pairs), line(lo, near_pairs)

    half = HD // 2
    freq = jnp.exp(jnp.arange(half, dtype=F32) * (-2.0 / HD * jnp.log(F32(1000000.0))))
    pos = lax.dynamic_slice(positions, (group * 512,), (512,)).astype(F32)
    pos = pos.reshape(4, 2, 64)
    pos = jnp.concatenate([pos[:, :, : PART[0]].reshape(4, -1), pos[:, :, PART[0] :].reshape(4, -1)], axis=1).reshape(512)
    angle = pos[:, None] * freq[None, :]
    cosine, sine = jnp.cos(angle), jnp.sin(angle)
    cos = jnp.concatenate([cosine, cosine], axis=1)
    sin = jnp.concatenate([-sine, sine], axis=1)
    rest = (k_bias.reshape(1, width), v_bias.reshape(1, width), cos, sin)

    wk, wv = in_hbm(k_weight), in_hbm(v_weight)
    together = lax.optimization_barrier

    def to_all(p):
        return [across(p, d) for d in (1, 2, 3)]

    (p0,) = wave("wave0", WHOLE, "whole", [own, own_s], wk, wv, rest)
    far1, near1, p0, lo, hi = together((far1, near1, p0, lo, hi))

    a0 = to_all(p0)
    far2, near2 = line(hi, far_pairs), line(hi, near_pairs)
    pieces1 = [(2, 0), (1, 0)]
    (p1,) = wave("wave1", pieces1, "pieces", [far1, sibling(far1), near1, sibling(near1)], wk, wv, rest)
    a0, far1, far2, near2, p1, own = together((a0, far1, far2, near2, p1, own))

    a1 = to_all(p1)
    middle, relay = line(own, middle_pairs), line(jnp.concatenate([far1, far2]), near_pairs)
    pieces2 = [(2, 1), (1, 1)]
    p2 = wave("wave2", pieces2, "pieces", [far2, sibling(far2), near2, sibling(near2)], wk, wv, rest, 2)
    a1, middle, relay, p2 = together((a1, middle, relay, p2))

    x2, y2 = [across(p, 1) for p in p2], [across(p, 2) for p in p2]
    sources = [middle, sibling(middle), relay, sibling(relay)]
    pieces3 = [(3, 0), (3, 1)]
    p3 = wave("wave3", pieces3, "relayed", sources, wk, wv, rest, 2)
    p3, x2, y2 = together((p3, x2, y2))
    x3, y3 = [across(p, 1) for p in p3], [across(p, 2) for p in p3]
    d2 = [across(x2[0], 2), across(y2[1], 1)]
    x3, y3, d2 = together((x3, y3, d2))
    d3 = [across(x3[0], 2), across(y3[1], 1)]

    units, arrays = [], []

    def arrived(pieces, split, got):
        total = sum(2 * PART[part] for _, part in pieces)
        each = total // split
        for d, parts in enumerate(got):
            row = 0
            for step, part in pieces:
                done = 0
                while done < 2 * PART[part]:
                    i = (row + done) // each
                    n = min(2 * PART[part] - done, (i + 1) * each - row - done)
                    units.append((d, step, PART_AT[part] + done, len(arrays) + i, row + done - i * each, n))
                    done += n
                row += done
            arrays.extend(parts)

    arrived(pieces2, 2, (p2, x2, y2, d2))
    arrived(pieces3, 2, (p3, x3, y3, d3))
    arrived(WHOLE, 1, [[one] for one in (p0, *a0)])
    arrived(pieces1, 1, [[one] for one in (p1, *a1)])
    return place(units, arrays, lengths, owner, 1024, width, 2048)


def solution(mesh):
    in_specs = (
        P(("group", "head"), None),
        P(),
        P(None, "head"),
        P("head"),
        P(None, "head"),
        P("head"),
        P(),
        P(),
        P(),
    )
    out_specs = (P("group", "head"), P("group", "head"))
    square = mesh.shape["group"] == 4 and mesh.shape["head"] == 8
    return jax.shard_map(
        pipelined if square else gathered, mesh=mesh, in_specs=in_specs, out_specs=out_specs, check_vma=False
    )
```

```python
import functools

import jax
import jax.numpy as jnp
from jax import lax
from jax.experimental import pallas as pl
from jax.experimental.pallas import tpu as pltpu
from jax.sharding import PartitionSpec as P

HD = 128
BF = jnp.bfloat16
F32 = jnp.float32
MIB = 1 << 20
VMEM = pltpu.VMEM
ANY = pltpu.HBM


def rotate(raw, pos):
    count = raw.shape[0]
    half = HD // 2
    x = raw.astype(jnp.float32).reshape(count, -1, HD)
    freq = jnp.exp(
        jnp.arange(half, dtype=jnp.float32) * (-2.0 / HD * jnp.log(jnp.float32(1000000.0)))
    )
    angle = pos.astype(jnp.float32)[:, None] * freq[None, :]
    cosine = jnp.cos(angle)[:, None, :]
    sine = jnp.sin(angle)[:, None, :]
    first = x[:, :, :half]
    second = x[:, :, half:]
    out = jnp.concatenate([first * cosine - second * sine, second * cosine + first * sine], axis=2)
    return out.reshape(count, -1).astype(jnp.bfloat16)


def cache_map(lengths, owner, group, cap):
    inside = owner == group
    own_len = jnp.where(inside, lengths, 0)
    start = jnp.cumsum(lengths) - lengths
    local = jnp.cumsum(own_len) - own_len
    row = jnp.arange(cap, dtype=jnp.int32)[:, None]
    match = inside[None, :] & (row >= local[None, :]) & (row < (local + lengths)[None, :])
    source = jnp.sum(jnp.where(match, start[None, :] + row - local[None, :], 0), axis=1)
    return (source, jnp.any(match, axis=1))


def gathered(hidden, norm_gain, k_weight, k_bias, v_weight, v_bias, positions, lengths, owner):
    rows = hidden.astype(jnp.float32)
    scale = lax.rsqrt(jnp.mean(rows * rows, axis=1, keepdims=True) + 1e-06)
    normed = (rows * scale * norm_gain.astype(jnp.float32)).astype(jnp.bfloat16)
    group_index = lax.axis_index("group")
    head_count = lax.axis_size("head")
    rows_dev = hidden.shape[0]
    width = k_weight.shape[1]
    cap = rows_dev * lax.axis_size("group") * head_count // 2
    piece = lax.all_gather(normed, "head", axis=0, tiled=True)
    key_raw = (
        jnp.dot(piece, k_weight, preferred_element_type=jnp.float32) + k_bias.astype(jnp.float32)
    ).astype(jnp.bfloat16)
    values = (
        jnp.dot(piece, v_weight, preferred_element_type=jnp.float32) + v_bias.astype(jnp.float32)
    ).astype(jnp.bfloat16)
    projected = jnp.concatenate([key_raw, values], axis=1)
    source, valid = cache_map(lengths, owner, group_index, cap)
    zero = jnp.zeros((), jnp.bfloat16)
    everything = lax.all_gather(projected, "group", axis=0, tiled=True)
    cache = jnp.where(valid[:, None], jnp.take(everything, source, axis=0), zero)
    key_cache = cache[:, :width]
    value_cache = cache[:, width:]
    row_pos = jnp.take(positions, source, axis=0)
    key_cache = jnp.where(valid[:, None], rotate(key_cache, row_pos), zero)
    return (key_cache, value_cache)


def norm_kernel(x_ref, gain_ref, out_ref, lo_ref, hi_ref):
    step = 16
    first = lo_ref.shape[0]
    gain = gain_ref[...].astype(F32)
    for at in range(0, x_ref.shape[0], step):
        x = x_ref[at : at + step, :].astype(F32)
        x = x * lax.rsqrt(jnp.mean(x * x, axis=1, keepdims=True) + 1e-06)
        y = [x[:, i * HD : (i + 1) * HD] * gain[i : i + 1, :] for i in range(gain.shape[0])]
        y = jnp.concatenate(y, axis=1).astype(BF)
        out_ref[at : at + step, :] = y
        if at < first:
            lo_ref[at : at + step, :] = y
        else:
            hi_ref[at - first : at - first + step, :] = y


def normalise(hidden, gain):
    rows, wide = hidden.shape
    return pl.pallas_call(
        norm_kernel,
        out_shape=tuple(VMEM((n, wide), BF) for n in (rows, *PART)),
        name="norm",
        cost_estimate=pl.CostEstimate(flops=rows * wide, bytes_accessed=rows, transcendentals=rows),
        compiler_params=pltpu.CompilerParams(vmem_limit_bytes=16 * MIB),
    )(hidden, gain.reshape(wide // HD, HD))


PART = (32, 32)
PART_AT = (0, 64)


def piece_at(step, part):
    return pl.multiple_of(((lax.axis_index("head") // 2) ^ step) * 128 + PART_AT[part], 32)


def rotation(pieces, cos, sin):
    return [
        jnp.concatenate([table[pl.ds(piece_at(*piece), 2 * PART[piece[1]]), :] for piece in pieces], axis=0)
        for table in (cos, sin)
    ]


def load_rows(x, pieces, sources, sem, start=True, wait=True):
    core = lax.axis_index("head") % 2
    base = 0
    for i, ((step, part), (own, sib, row)) in enumerate(zip(pieces, sources)):
        n = PART[part]
        for j, src in enumerate((own, sib)):
            at = pl.multiple_of(base + (core ^ j) * n, 16)
            copy = pltpu.make_async_copy(src.at[pl.ds(row, n)], x.at[pl.ds(at, n)], sem.at[2 * i + j])
            if start:
                copy.start()
            if wait:
                copy.wait()
        base += 2 * n


def turn(raw, c, s):
    raw = raw.astype(BF).astype(F32)
    heads = []
    for h in range(raw.shape[1] // HD):
        one = raw[:, h * HD : (h + 1) * HD]
        heads.append(one * c + pltpu.roll(one, HD // 2, axis=1) * s)
    return jnp.concatenate(heads, axis=1).astype(BF)


WHOLE = [(0, 0), (0, 1)]


def both(own, sib):
    return [(own, sib, 0), (own, sib, PART[0])]


def wave_kernel(pieces, kind, mode, count, *refs):
    sources = refs[:count]
    wk, wv, kb, vb, cos, sin = refs[count : count + 6]
    outs, x, sem, scratch = list(refs[count + 6 :]), None, None, []
    if mode == "use":
        x, sem = outs[-2:]
        outs = outs[:-2]
        kept = (wk, wv)
    elif mode == "keep":
        x, sem, wsem = outs[-3:]
        kept = outs[-5:-3]
        outs = outs[:-5]
    else:
        x, sem, wsem, blocks = outs[-4:]
        outs = outs[:-4]
    deep, width = wk.shape
    tile = 256
    each = width // tile
    total = 2 * each
    half = deep // 2

    def block(i):
        if mode == "stream":
            return blocks.at[i % blocks.shape[0]]
        return kept[i // each].at[:, pl.ds(i % each * tile, tile)]

    copies = []
    if mode != "use":
        for i in range(total):
            cols = pl.ds(i % each * tile, tile)
            copies.append(
                [
                    pltpu.make_async_copy(
                        (wk, wv)[i // each].at[pl.ds(j * half, half), cols],
                        block(i).at[pl.ds(j * half, half)],
                        wsem.at[2 * i + j],
                    )
                    for j in range(2)
                ]
            )

    def fetch(i):
        for copy in copies[i]:
            copy.start()

    load = functools.partial(load_rows, x, pieces)
    if kind == "relayed":
        chip = lax.axis_index("head") // 2
        at_end = (chip == 0) | (chip == 3)
        rows = both(*sources[:2])
        ends = both(*sources[2:])
        pl.when(jnp.logical_not(at_end))(lambda: load(rows, sem, wait=False))
        pl.when(at_end)(lambda: load(ends, sem, wait=False))
    else:
        rows = both(*sources) if kind == "whole" else [(sources[i], sources[i + 1], 0) for i in range(0, count, 2)]
        load(rows, sem, wait=False)
    ahead = {"use": 0, "keep": total, "stream": DEPTH}[mode]
    for i in range(ahead):
        fetch(i)
    c, s = rotation(pieces, cos, sin)
    load(rows, sem, start=False)
    part = x.shape[0] // len(outs)
    for i in range(total):
        if copies:
            for copy in copies[i]:
                copy.wait()
        raw = jnp.dot(x[...], block(i)[...], preferred_element_type=F32)
        if i < each:
            y = turn(raw + kb[:, i * tile : (i + 1) * tile].astype(F32), c, s)
        else:
            at = (i - each) * tile
            y = (raw + vb[:, at : at + tile].astype(F32)).astype(BF)
        for k, out in enumerate(outs):
            out[:, i * tile : (i + 1) * tile] = y[k * part : (k + 1) * part]
        if mode == "stream" and i + DEPTH < total:
            fetch(i + DEPTH)


DEPTH = 3


def cost(m, deep, width, weights):
    return pl.CostEstimate(flops=m * width, bytes_accessed=2 * m * width, transcendentals=0)


def in_hbm(x):
    return pltpu.with_memory_space_constraint(x, pltpu.HBM)


def wave(name, pieces, kind, sources, wk, wv, rest, split=1, mode="stream"):
    deep, width = wk.shape
    m = sum(2 * PART[part] for _, part in pieces)
    tile = 256
    full = pl.BlockSpec(memory_space=VMEM)
    hbm = pl.BlockSpec(memory_space=ANY)
    scratch = [VMEM((m, deep), BF), pltpu.SemaphoreType.DMA((2 * len(pieces),))]
    outs = [VMEM((m // split, 2 * width), BF)] * split
    if mode != "use":
        scratch.append(pltpu.SemaphoreType.DMA((4 * width // tile,)))
    if mode == "stream":
        scratch.append(VMEM((DEPTH, deep, tile), BF))
    if mode == "keep":
        outs += [VMEM((deep, width), BF)] * 2
    return pl.pallas_call(
        functools.partial(wave_kernel, pieces, kind, mode, len(sources)),
        out_shape=outs,
        in_specs=[hbm] * len(sources) + [full if mode == "use" else hbm] * 2 + [full] * 4,
        out_specs=[full] * len(outs),
        scratch_shapes=scratch,
        name=name,
        cost_estimate=cost(m, deep, width, True),
        compiler_params=pltpu.CompilerParams(vmem_limit_bytes=(18 if mode == "stream" else 6) * MIB),
    )(*sources, wk, wv, *rest)


def place_kernel(units, lengths, owner, *refs):
    count = max(unit[3] for unit in units) + 1
    sources = refs[:count]
    key_out, value_out, rows = refs[count:]
    width = key_out.shape[1]
    group = lax.axis_index("group")
    chip = lax.axis_index("head") // 2
    for d, step, at, a, row, n in units:
        whose = d[0] if isinstance(d, tuple) else group ^ d
        to = pl.multiple_of(whose * 512 + (chip ^ step) * 128 + at, 16)
        rows[pl.ds(to, n), :] = sources[a][row : row + n, :]
    key_out[...] = jnp.zeros_like(key_out)
    value_out[...] = jnp.zeros_like(value_out)
    tile, window = 128, 256
    total = rows.shape[0]

    def request(q, carry):
        start, local = carry
        length = lengths[q]
        mine = owner[q] == group

        @pl.when(mine)
        def _():
            def step(t, c):
                top = pl.multiple_of(t * tile, tile)
                base = start + top - local
                at = pl.multiple_of(jnp.clip((base >> 7) << 7, 0, total - window), 128)
                lane = lax.broadcasted_iota(jnp.int32, (tile, window), 1)
                p = lane & 127
                first, second = PART
                stay = (p < first) | (p >= 128 - second)
                src = at + lane + jnp.where(stay, 0, jnp.where(p < 2 * first, second, -first))
                dst = base + lax.broadcasted_iota(jnp.int32, (tile, window), 0)
                hit = (src == dst) & (src >= start) & (src < start + length)
                pick = jnp.where(hit, 1.0, 0.0).astype(BF)
                for part, out in ((0, key_out), (1, value_out)):
                    moved = jnp.dot(pick, rows[pl.ds(at, window), part * width : (part + 1) * width], preferred_element_type=F32)
                    out[pl.ds(top, tile), :] += moved.astype(BF)
                return c

            lax.fori_loop(local // tile, (local + length - 1) // tile + 1, step, 0)

        return (start + length, local + jnp.where(mine, length, 0))

    lax.fori_loop(0, lengths.shape[0], request, (jnp.int32(0), jnp.int32(0)))


def place(units, arrays, lengths, owner, cap, width, total):
    out = jax.ShapeDtypeStruct((cap, width), BF)
    smem = pl.BlockSpec(memory_space=pltpu.SMEM)
    full = pl.BlockSpec(memory_space=VMEM)
    return pl.pallas_call(
        functools.partial(place_kernel, units),
        out_shape=(out, out),
        in_specs=[smem, smem] + [full] * len(arrays),
        out_specs=(full, full),
        scratch_shapes=[VMEM((total, 2 * width), BF)],
        name="place",
        cost_estimate=pl.CostEstimate(flops=0, bytes_accessed=20 * MIB, transcendentals=0),
        compiler_params=pltpu.CompilerParams(vmem_limit_bytes=28 * MIB),
    )(lengths, owner, *arrays)


def pipelined(hidden, norm_gain, k_weight, k_bias, v_weight, v_bias, positions, lengths, owner):
    width = k_weight.shape[1]
    group = lax.axis_index("group")

    def line(x, pairs):
        return lax.ppermute(x, "head", [(2 * a + c, 2 * b + c) for a, b in pairs for c in range(2)])

    def sibling(x):
        return lax.ppermute(x, "head", [(i, i ^ 1) for i in range(8)])

    def across(x, bit):
        return lax.ppermute(x, "group", [(i, i ^ bit) for i in range(4)])

    far_pairs = [(0, 2), (1, 3), (2, 0), (3, 1)]
    near_pairs = [(0, 1), (1, 0), (2, 3), (3, 2)]
    middle_pairs = [(1, 2), (2, 1)]

    def after(x, *done):
        return lax.optimization_barrier((x,) + done)[0]

    own, lo, hi = normalise(hidden, norm_gain)
    own_s = sibling(own)
    far1, near1 = line(lo, far_pairs), line(lo, near_pairs)

    half = HD // 2
    freq = jnp.exp(jnp.arange(half, dtype=F32) * (-2.0 / HD * jnp.log(F32(1000000.0))))
    pos = lax.dynamic_slice(positions, (group * 512,), (512,)).astype(F32)
    pos = pos.reshape(4, 2, 64)
    pos = jnp.concatenate([pos[:, :, : PART[0]].reshape(4, -1), pos[:, :, PART[0] :].reshape(4, -1)], axis=1).reshape(512)
    angle = pos[:, None] * freq[None, :]
    cosine, sine = jnp.cos(angle), jnp.sin(angle)
    cos = jnp.concatenate([cosine, cosine], axis=1)
    sin = jnp.concatenate([-sine, sine], axis=1)
    rest = (k_bias.reshape(1, width), v_bias.reshape(1, width), cos, sin)

    wk, wv = in_hbm(k_weight), in_hbm(v_weight)
    kk, kv = (pltpu.with_memory_space_constraint(w, VMEM) for w in (k_weight, v_weight))
    together = lax.optimization_barrier
    (p0,) = wave("wave0", WHOLE, "whole", [own, own_s], wk, wv, rest)
    far1, near1, p0, lo, hi, own = together((far1, near1, p0, lo, hi, own))

    far2, near2 = line(hi, far_pairs), line(hi, near_pairs)
    x0, y0 = across(p0, 1), across(p0, 2)
    pieces1 = [(2, 0), (1, 0)]
    (p1,) = wave("wave1", pieces1, "pieces", [far1, sibling(far1), near1, sibling(near1)], kk, kv, rest, 1, "use")
    p1, x0, y0 = together((p1, x0, y0))
    x1, y1 = across(p1, 1), across(p1, 2)
    x0, x1, y1, far1, far2, near2, p1, own = together((x0, x1, y1, far1, far2, near2, p1, own))

    middle, relay = line(own, middle_pairs), line(jnp.concatenate([far1, far2]), near_pairs)
    d0, d1 = across(x0, 2), across(y1, 1)
    pieces2 = [(2, 1), (1, 1)]
    p2 = wave("wave2", pieces2, "pieces", [far2, sibling(far2), near2, sibling(near2)], kk, kv, rest, 2, "use")
    d0, d1, *p2 = together((d0, d1, *p2))
    x2, y2 = [across(p, 1) for p in p2], [across(p, 2) for p in p2]
    x2, y2, middle, relay = together((x2, y2, middle, relay))

    d2 = [across(x2[0], 2), across(y2[1], 1)]
    sources = [middle, sibling(middle), relay, sibling(relay)]
    pieces3 = [(3, 0), (3, 1)]
    p3 = wave("wave3", pieces3, "relayed", sources, kk, kv, rest, 2, "use")
    p3, d2 = together((p3, d2))
    x3, y3 = [across(p, 1) for p in p3], [across(p, 2) for p in p3]
    d3 = [across(x3[0], 2), across(y3[1], 1)]

    units, arrays = [], []

    def arrived(pieces, split, got):
        total = sum(2 * PART[part] for _, part in pieces)
        each = total // split
        for d, parts in enumerate(got):
            row = 0
            for step, part in pieces:
                done = 0
                while done < 2 * PART[part]:
                    i = (row + done) // each
                    n = min(2 * PART[part] - done, (i + 1) * each - row - done)
                    units.append((d, step, PART_AT[part] + done, len(arrays) + i, row + done - i * each, n))
                    done += n
                row += done
            arrays.extend(parts)

    arrived(WHOLE, 1, [[one] for one in (p0, x0, y0, d0)])
    arrived(pieces1, 1, [[one] for one in (p1, x1, y1, d1)])
    arrived(pieces2, 2, (p2, x2, y2, d2))
    arrived(pieces3, 2, (p3, x3, y3, d3))
    return place(units, arrays, lengths, owner, 1024, width, 2048)


def solution(mesh):
    in_specs = (
        P(("group", "head"), None),
        P(),
        P(None, "head"),
        P("head"),
        P(None, "head"),
        P("head"),
        P(),
        P(),
        P(),
    )
    out_specs = (P("group", "head"), P("group", "head"))
    square = mesh.shape["group"] == 4 and mesh.shape["head"] == 8
    return jax.shard_map(
        pipelined if square else gathered, mesh=mesh, in_specs=in_specs, out_specs=out_specs, check_vma=False
    )
```

```python
import functools

import jax
import jax.numpy as jnp
from jax import lax
from jax.experimental import pallas as pl
from jax.experimental.pallas import tpu as pltpu
from jax.sharding import PartitionSpec as P

HD = 128
BF = jnp.bfloat16
F32 = jnp.float32
MIB = 1 << 20
VMEM = pltpu.VMEM
ANY = pltpu.HBM


def rotate(raw, pos):
    count = raw.shape[0]
    half = HD // 2
    x = raw.astype(jnp.float32).reshape(count, -1, HD)
    freq = jnp.exp(
        jnp.arange(half, dtype=jnp.float32) * (-2.0 / HD * jnp.log(jnp.float32(1000000.0)))
    )
    angle = pos.astype(jnp.float32)[:, None] * freq[None, :]
    cosine = jnp.cos(angle)[:, None, :]
    sine = jnp.sin(angle)[:, None, :]
    first = x[:, :, :half]
    second = x[:, :, half:]
    out = jnp.concatenate([first * cosine - second * sine, second * cosine + first * sine], axis=2)
    return out.reshape(count, -1).astype(jnp.bfloat16)


def cache_map(lengths, owner, group, cap):
    inside = owner == group
    own_len = jnp.where(inside, lengths, 0)
    start = jnp.cumsum(lengths) - lengths
    local = jnp.cumsum(own_len) - own_len
    row = jnp.arange(cap, dtype=jnp.int32)[:, None]
    match = inside[None, :] & (row >= local[None, :]) & (row < (local + lengths)[None, :])
    source = jnp.sum(jnp.where(match, start[None, :] + row - local[None, :], 0), axis=1)
    return (source, jnp.any(match, axis=1))


def gathered(hidden, norm_gain, k_weight, k_bias, v_weight, v_bias, positions, lengths, owner):
    rows = hidden.astype(jnp.float32)
    scale = lax.rsqrt(jnp.mean(rows * rows, axis=1, keepdims=True) + 1e-06)
    normed = (rows * scale * norm_gain.astype(jnp.float32)).astype(jnp.bfloat16)
    group_index = lax.axis_index("group")
    head_count = lax.axis_size("head")
    rows_dev = hidden.shape[0]
    width = k_weight.shape[1]
    cap = rows_dev * lax.axis_size("group") * head_count // 2
    piece = lax.all_gather(normed, "head", axis=0, tiled=True)
    key_raw = (
        jnp.dot(piece, k_weight, preferred_element_type=jnp.float32) + k_bias.astype(jnp.float32)
    ).astype(jnp.bfloat16)
    values = (
        jnp.dot(piece, v_weight, preferred_element_type=jnp.float32) + v_bias.astype(jnp.float32)
    ).astype(jnp.bfloat16)
    projected = jnp.concatenate([key_raw, values], axis=1)
    source, valid = cache_map(lengths, owner, group_index, cap)
    zero = jnp.zeros((), jnp.bfloat16)
    everything = lax.all_gather(projected, "group", axis=0, tiled=True)
    cache = jnp.where(valid[:, None], jnp.take(everything, source, axis=0), zero)
    key_cache = cache[:, :width]
    value_cache = cache[:, width:]
    row_pos = jnp.take(positions, source, axis=0)
    key_cache = jnp.where(valid[:, None], rotate(key_cache, row_pos), zero)
    return (key_cache, value_cache)


def norm_kernel(x_hbm, gain_hbm, out_ref, lo_ref, hi_ref, x_ref, gain_ref, sem):
    step = 16
    first = lo_ref.shape[0]
    rows = x_ref.shape[0]
    gain_copy = pltpu.make_async_copy(gain_hbm, gain_ref, sem.at[0])
    copies = [
        pltpu.make_async_copy(x_hbm.at[pl.ds(at, step)], x_ref.at[pl.ds(at, step)], sem.at[1 + at // step])
        for at in range(0, rows, step)
    ]
    for copy in copies:
        copy.start()
    gain_copy.start()
    gain_copy.wait()
    gain = gain_ref[...].astype(F32)
    for at, copy in zip(range(0, rows, step), copies):
        copy.wait()
        x = x_ref[at : at + step, :].astype(F32)
        x = x * lax.rsqrt(jnp.mean(x * x, axis=1, keepdims=True) + 1e-06)
        y = [x[:, i * HD : (i + 1) * HD] * gain[i : i + 1, :] for i in range(gain.shape[0])]
        y = jnp.concatenate(y, axis=1).astype(BF)
        out_ref[at : at + step, :] = y
        if at < first:
            lo_ref[at : at + step, :] = y
        else:
            hi_ref[at - first : at - first + step, :] = y


def normalise(hidden, gain):
    rows, wide = hidden.shape
    hbm = pl.BlockSpec(memory_space=ANY)
    return pl.pallas_call(
        norm_kernel,
        out_shape=(VMEM((rows, wide), BF), VMEM((PART[0], wide), BF), pltpu.HBM((PART[1], wide), BF)),
        in_specs=[hbm, hbm],
        scratch_shapes=[
            VMEM((rows, wide), BF),
            VMEM((wide // HD, HD), BF),
            pltpu.SemaphoreType.DMA((1 + rows // 16,)),
        ],
        name="norm",
        cost_estimate=pl.CostEstimate(flops=rows * wide, bytes_accessed=rows, transcendentals=rows),
        compiler_params=pltpu.CompilerParams(vmem_limit_bytes=16 * MIB),
    )(in_hbm(hidden), in_hbm(gain.reshape(wide // HD, HD)))


PART = (32, 32)
PART_AT = (0, 64)


def piece_at(step, part):
    return pl.multiple_of(((lax.axis_index("head") // 2) ^ step) * 128 + PART_AT[part], 32)


def rotation(pieces, cos, sin):
    return [
        jnp.concatenate([table[pl.ds(piece_at(*piece), 2 * PART[piece[1]]), :] for piece in pieces], axis=0)
        for table in (cos, sin)
    ]


def load_rows(x, pieces, sources, sem, start=True, wait=True):
    core = lax.axis_index("head") % 2
    base = 0
    for i, ((step, part), (own, sib, row)) in enumerate(zip(pieces, sources)):
        n = PART[part]
        for j, src in enumerate((own, sib)):
            at = pl.multiple_of(base + (core ^ j) * n, 16)
            copy = pltpu.make_async_copy(src.at[pl.ds(row, n)], x.at[pl.ds(at, n)], sem.at[2 * i + j])
            if start:
                copy.start()
            if wait:
                copy.wait()
        base += 2 * n


def turn(raw, c, s):
    raw = raw.astype(BF).astype(F32)
    heads = []
    for h in range(raw.shape[1] // HD):
        one = raw[:, h * HD : (h + 1) * HD]
        heads.append(one * c + pltpu.roll(one, HD // 2, axis=1) * s)
    return jnp.concatenate(heads, axis=1).astype(BF)


WHOLE = [(0, 0), (0, 1)]


def both(own, sib):
    return [(own, sib, 0), (own, sib, PART[0])]


def wave_kernel(pieces, kind, mode, count, *refs):
    sources = refs[:count]
    wk, wv, kb, vb, cos, sin = refs[count : count + 6]
    outs, x, sem, scratch = list(refs[count + 6 :]), None, None, []
    if mode == "use":
        x, sem = outs[-2:]
        outs = outs[:-2]
        kept = (wk, wv)
    elif mode == "keep":
        x, sem, wsem = outs[-3:]
        kept = outs[-5:-3]
        outs = outs[:-5]
    else:
        x, sem, wsem, blocks = outs[-4:]
        outs = outs[:-4]
    deep, width = wk.shape
    tile = 256
    each = width // tile
    total = 2 * each
    half = deep // 2

    def block(i):
        if mode == "stream":
            return blocks.at[i % blocks.shape[0]]
        return kept[i // each].at[:, pl.ds(i % each * tile, tile)]

    copies = []
    if mode != "use":
        for i in range(total):
            cols = pl.ds(i % each * tile, tile)
            copies.append(
                [
                    pltpu.make_async_copy(
                        (wk, wv)[i // each].at[pl.ds(j * half, half), cols],
                        block(i).at[pl.ds(j * half, half)],
                        wsem.at[2 * i + j],
                    )
                    for j in range(2)
                ]
            )

    def fetch(i):
        for copy in copies[i]:
            copy.start()

    load = functools.partial(load_rows, x, pieces)
    if kind == "relayed":
        chip = lax.axis_index("head") // 2
        at_end = (chip == 0) | (chip == 3)
        rows = both(*sources[:2])
        ends = both(*sources[2:])
        pl.when(jnp.logical_not(at_end))(lambda: load(rows, sem, wait=False))
        pl.when(at_end)(lambda: load(ends, sem, wait=False))
    else:
        rows = both(*sources) if kind == "whole" else [(sources[i], sources[i + 1], 0) for i in range(0, count, 2)]
        load(rows, sem, wait=False)
    ahead = {"use": 0, "keep": total, "stream": DEPTH}[mode]
    for i in range(ahead):
        fetch(i)
    c, s = rotation(pieces, cos, sin)
    load(rows, sem, start=False)
    part = x.shape[0] // len(outs)
    for i in range(total):
        if copies:
            for copy in copies[i]:
                copy.wait()
        raw = jnp.dot(x[...], block(i)[...], preferred_element_type=F32)
        if i < each:
            y = turn(raw + kb[:, i * tile : (i + 1) * tile].astype(F32), c, s)
        else:
            at = (i - each) * tile
            y = (raw + vb[:, at : at + tile].astype(F32)).astype(BF)
        for k, out in enumerate(outs):
            out[:, i * tile : (i + 1) * tile] = y[k * part : (k + 1) * part]
        if mode == "stream" and i + DEPTH < total:
            fetch(i + DEPTH)


DEPTH = 3


def cost(m, deep, width, weights):
    return pl.CostEstimate(flops=m * width, bytes_accessed=2 * m * width, transcendentals=0)


def in_hbm(x):
    return pltpu.with_memory_space_constraint(x, pltpu.HBM)


def wave(name, pieces, kind, sources, wk, wv, rest, split=1, mode="stream"):
    deep, width = wk.shape
    m = sum(2 * PART[part] for _, part in pieces)
    tile = 256
    full = pl.BlockSpec(memory_space=VMEM)
    hbm = pl.BlockSpec(memory_space=ANY)
    scratch = [VMEM((m, deep), BF), pltpu.SemaphoreType.DMA((2 * len(pieces),))]
    outs = [VMEM((m // split, 2 * width), BF)] * split
    if mode != "use":
        scratch.append(pltpu.SemaphoreType.DMA((4 * width // tile,)))
    if mode == "stream":
        scratch.append(VMEM((DEPTH, deep, tile), BF))
    if mode == "keep":
        outs += [VMEM((deep, width), BF)] * 2
    return pl.pallas_call(
        functools.partial(wave_kernel, pieces, kind, mode, len(sources)),
        out_shape=outs,
        in_specs=[hbm] * len(sources) + [full if mode == "use" else hbm] * 2 + [full] * 4,
        out_specs=[full] * len(outs),
        scratch_shapes=scratch,
        name=name,
        cost_estimate=cost(m, deep, width, True),
        compiler_params=pltpu.CompilerParams(vmem_limit_bytes=(18 if mode == "stream" else 6) * MIB),
    )(*sources, wk, wv, *rest)


def place_kernel(units, own, lengths, owner, *refs):
    count = max(unit[3] for unit in units) + 1
    sources = refs[:count]
    key_out, value_out, rows, cache, held, sem, out_sem = refs[count:]
    width = key_out.shape[1]
    group = lax.axis_index("group")
    chip = lax.axis_index("head") // 2
    copies = []

    def target(d, step, at, n):
        to = pl.multiple_of((group ^ d) * 512 + (chip ^ step) * 128 + at, 16)
        return rows.at[pl.ds(to, n)]

    for d, step, at, a, row, n in units:
        if a in own:
            copies.append(
                pltpu.make_async_copy(sources[a].at[pl.ds(row, n)], target(d, step, at, n), sem.at[len(copies)])
            )
            copies[-1].start()
    for d, step, at, a, row, n in units:
        if a not in own:
            target(d, step, at, n)[...] = sources[a][row : row + n, :]

    def request(q, carry):
        start, local, mine = carry
        length = lengths[q]
        hit = owner[q] == group

        @pl.when(hit)
        def _():
            held[0, mine] = start
            held[1, mine] = local
            held[2, mine] = length

        return (start + length, local + jnp.where(hit, length, 0), mine + jnp.where(hit, 1, 0))

    zero = jnp.int32(0)
    _, _, requests = lax.fori_loop(0, lengths.shape[0], request, (zero, zero, zero))
    for copy in copies:
        copy.wait()
    tile, window = 128, 256
    total = rows.shape[0]
    tiles = cache.shape[0] // tile

    def writes(t):
        top = pl.multiple_of(t * tile, tile)
        return [
            pltpu.make_async_copy(
                cache.at[pl.ds(top, tile), pl.ds(part * width, width)], out.at[pl.ds(top, tile)], out_sem.at[t, part]
            )
            for part, out in enumerate((key_out, value_out))
        ]

    def fill(t, carry):
        top = pl.multiple_of(t * tile, tile)
        cache[pl.ds(top, tile), :] = jnp.zeros((tile, cache.shape[1]), BF)

        def add(q, c):
            start, local, length = held[0, q], held[1, q], held[2, q]

            @pl.when((local < top + tile) & (local + length > top))
            def _():
                base = start + top - local
                at = pl.multiple_of(jnp.clip((base >> 7) << 7, 0, total - window), 128)
                lane = lax.broadcasted_iota(jnp.int32, (tile, window), 1)
                p = lane & 127
                first, second = PART
                stay = (p < first) | (p >= 128 - second)
                src = at + lane + jnp.where(stay, 0, jnp.where(p < 2 * first, second, -first))
                dst = base + lax.broadcasted_iota(jnp.int32, (tile, window), 0)
                hit = (src == dst) & (src >= start) & (src < start + length)
                pick = jnp.where(hit, 1.0, 0.0).astype(BF)
                for i in range(2):
                    cols = slice(i * width, (i + 1) * width)
                    moved = jnp.dot(pick, rows[pl.ds(at, window), cols], preferred_element_type=F32)
                    cache[pl.ds(top, tile), cols] += moved.astype(BF)

            return c

        lax.fori_loop(0, requests, add, 0)
        for write in writes(t):
            write.start()
        return carry

    lax.fori_loop(0, tiles, fill, 0)

    def finish(t, carry):
        for write in writes(t):
            write.wait()
        return carry

    lax.fori_loop(0, tiles, finish, 0)


def place(units, own, arrays, lengths, owner, cap, width, total):
    out = jax.ShapeDtypeStruct((cap, width), BF)
    smem = pl.BlockSpec(memory_space=pltpu.SMEM)
    full = pl.BlockSpec(memory_space=VMEM)
    hbm = pl.BlockSpec(memory_space=ANY)
    return pl.pallas_call(
        functools.partial(place_kernel, units, own),
        out_shape=(out, out),
        in_specs=[smem, smem] + [hbm if i in own else full for i in range(len(arrays))],
        out_specs=(hbm, hbm),
        scratch_shapes=[
            VMEM((total, 2 * width), BF),
            VMEM((cap, 2 * width), BF),
            pltpu.SMEM((3, lengths.shape[0]), jnp.int32),
            pltpu.SemaphoreType.DMA((sum(unit[3] in own for unit in units),)),
            pltpu.SemaphoreType.DMA((cap // 128, 2)),
        ],
        name="place",
        cost_estimate=pl.CostEstimate(flops=0, bytes_accessed=20 * MIB, transcendentals=0),
        compiler_params=pltpu.CompilerParams(vmem_limit_bytes=24 * MIB),
    )(lengths, owner, *arrays)


def pipelined(hidden, norm_gain, k_weight, k_bias, v_weight, v_bias, positions, lengths, owner):
    width = k_weight.shape[1]
    group = lax.axis_index("group")

    def line(x, pairs):
        return lax.ppermute(x, "head", [(2 * a + c, 2 * b + c) for a, b in pairs for c in range(2)])

    def sibling(x):
        return lax.ppermute(x, "head", [(i, i ^ 1) for i in range(8)])

    def across(x, bit):
        return lax.ppermute(x, "group", [(i, i ^ bit) for i in range(4)])

    far_pairs = [(0, 2), (1, 3), (2, 0), (3, 1)]
    near_pairs = [(0, 1), (1, 0), (2, 3), (3, 2)]
    middle_pairs = [(1, 2), (2, 1)]

    def after(x, *done):
        return lax.optimization_barrier((x,) + done)[0]

    own, lo, hi = normalise(hidden, norm_gain)
    own_s = sibling(own)
    far1, near1 = line(lo, far_pairs), line(lo, near_pairs)

    half = HD // 2
    freq = jnp.exp(jnp.arange(half, dtype=F32) * (-2.0 / HD * jnp.log(F32(1000000.0))))
    pos = lax.dynamic_slice(positions, (group * 512,), (512,)).astype(F32)
    pos = pos.reshape(4, 2, 64)
    pos = jnp.concatenate([pos[:, :, : PART[0]].reshape(4, -1), pos[:, :, PART[0] :].reshape(4, -1)], axis=1).reshape(512)
    angle = pos[:, None] * freq[None, :]
    cosine, sine = jnp.cos(angle), jnp.sin(angle)
    cos = jnp.concatenate([cosine, cosine], axis=1)
    sin = jnp.concatenate([-sine, sine], axis=1)
    rest = (k_bias.reshape(1, width), v_bias.reshape(1, width), cos, sin)

    wk, wv = in_hbm(k_weight), in_hbm(v_weight)
    kk, kv = (pltpu.with_memory_space_constraint(w, VMEM) for w in (k_weight, v_weight))
    together = lax.optimization_barrier
    (p0,) = wave("wave0", WHOLE, "whole", [own, own_s], wk, wv, rest)
    far1, near1, p0, lo, hi, own = together((far1, near1, p0, lo, hi, own))

    far2, near2 = line(hi, far_pairs), line(hi, near_pairs)
    x0, y0 = across(p0, 1), across(p0, 2)
    pieces1 = [(2, 0), (1, 0)]
    (p1,) = wave("wave1", pieces1, "pieces", [far1, sibling(far1), near1, sibling(near1)], kk, kv, rest, 1, "use")
    p1, x0, y0 = together((p1, x0, y0))
    x1, y1 = across(p1, 1), across(p1, 2)
    x0, x1, y1, far1, far2, near2, p1, own = together((x0, x1, y1, far1, far2, near2, p1, own))

    middle, relay = line(own, middle_pairs), line(jnp.concatenate([far1, far2]), near_pairs)
    d0, d1 = across(x0, 2), across(y1, 1)
    pieces2 = [(2, 1), (1, 1)]
    p2 = wave("wave2", pieces2, "pieces", [far2, sibling(far2), near2, sibling(near2)], kk, kv, rest, 2, "use")
    d0, d1, *p2 = together((d0, d1, *p2))
    x2, y2 = [across(p, 1) for p in p2], [across(p, 2) for p in p2]
    x2, y2, middle, relay = together((x2, y2, middle, relay))

    d2 = [across(x2[0], 2), across(y2[1], 1)]
    sources = [middle, sibling(middle), relay, sibling(relay)]
    pieces3 = [(3, 0), (3, 1)]
    p3 = wave("wave3", pieces3, "relayed", sources, kk, kv, rest, 2, "use")
    p3, d2 = together((p3, d2))
    x3, y3 = [across(p, 1) for p in p3], [across(p, 2) for p in p3]
    d3 = [across(x3[0], 2), across(y3[1], 1)]

    units, arrays, mine = [], [], set()

    def arrived(pieces, split, got, early=False):
        total = sum(2 * PART[part] for _, part in pieces)
        each = total // split
        for d, parts in enumerate(got):
            row = 0
            if d == 0:
                mine.update(range(len(arrays), len(arrays) + split))
            if early and d in (1, 2):
                mine.add(len(arrays) + split - 1)
                parts = [*parts[:-1], in_hbm(parts[-1])]
            for step, part in pieces:
                done = 0
                while done < 2 * PART[part]:
                    i = (row + done) // each
                    n = min(2 * PART[part] - done, (i + 1) * each - row - done)
                    units.append((d, step, PART_AT[part] + done, len(arrays) + i, row + done - i * each, n))
                    done += n
                row += done
            arrays.extend(parts)

    arrived(WHOLE, 1, [[one] for one in (p0, x0, y0, d0)])
    arrived(pieces1, 1, [[one] for one in (p1, x1, y1, d1)])
    arrived(pieces2, 2, (p2, x2, y2, d2), True)
    arrived(pieces3, 2, (p3, x3, y3, d3))
    return place(units, sorted(mine), arrays, lengths, owner, 1024, width, 2048)


def solution(mesh):
    in_specs = (
        P(("group", "head"), None),
        P(),
        P(None, "head"),
        P("head"),
        P(None, "head"),
        P("head"),
        P(),
        P(),
        P(),
    )
    out_specs = (P("group", "head"), P("group", "head"))
    square = mesh.shape["group"] == 4 and mesh.shape["head"] == 8
    return jax.shard_map(
        pipelined if square else gathered, mesh=mesh, in_specs=in_specs, out_specs=out_specs, check_vma=False
    )
```

```python
import functools

import jax
import jax.numpy as jnp
from jax import lax
from jax.experimental import pallas as pl
from jax.experimental.pallas import tpu as pltpu
from jax.sharding import PartitionSpec as P

HD = 128
BF = jnp.bfloat16
F32 = jnp.float32
MIB = 1 << 20
VMEM = pltpu.VMEM
ANY = pltpu.HBM


def rotate(raw, pos):
    count = raw.shape[0]
    half = HD // 2
    x = raw.astype(jnp.float32).reshape(count, -1, HD)
    freq = jnp.exp(
        jnp.arange(half, dtype=jnp.float32) * (-2.0 / HD * jnp.log(jnp.float32(1000000.0)))
    )
    angle = pos.astype(jnp.float32)[:, None] * freq[None, :]
    cosine = jnp.cos(angle)[:, None, :]
    sine = jnp.sin(angle)[:, None, :]
    first = x[:, :, :half]
    second = x[:, :, half:]
    out = jnp.concatenate([first * cosine - second * sine, second * cosine + first * sine], axis=2)
    return out.reshape(count, -1).astype(jnp.bfloat16)


def cache_map(lengths, owner, group, cap):
    inside = owner == group
    own_len = jnp.where(inside, lengths, 0)
    start = jnp.cumsum(lengths) - lengths
    local = jnp.cumsum(own_len) - own_len
    row = jnp.arange(cap, dtype=jnp.int32)[:, None]
    match = inside[None, :] & (row >= local[None, :]) & (row < (local + lengths)[None, :])
    source = jnp.sum(jnp.where(match, start[None, :] + row - local[None, :], 0), axis=1)
    return (source, jnp.any(match, axis=1))


def gathered(hidden, norm_gain, k_weight, k_bias, v_weight, v_bias, positions, lengths, owner):
    rows = hidden.astype(jnp.float32)
    scale = lax.rsqrt(jnp.mean(rows * rows, axis=1, keepdims=True) + 1e-06)
    normed = (rows * scale * norm_gain.astype(jnp.float32)).astype(jnp.bfloat16)
    group_index = lax.axis_index("group")
    head_count = lax.axis_size("head")
    rows_dev = hidden.shape[0]
    width = k_weight.shape[1]
    cap = rows_dev * lax.axis_size("group") * head_count // 2
    piece = lax.all_gather(normed, "head", axis=0, tiled=True)
    key_raw = (
        jnp.dot(piece, k_weight, preferred_element_type=jnp.float32) + k_bias.astype(jnp.float32)
    ).astype(jnp.bfloat16)
    values = (
        jnp.dot(piece, v_weight, preferred_element_type=jnp.float32) + v_bias.astype(jnp.float32)
    ).astype(jnp.bfloat16)
    projected = jnp.concatenate([key_raw, values], axis=1)
    source, valid = cache_map(lengths, owner, group_index, cap)
    zero = jnp.zeros((), jnp.bfloat16)
    everything = lax.all_gather(projected, "group", axis=0, tiled=True)
    cache = jnp.where(valid[:, None], jnp.take(everything, source, axis=0), zero)
    key_cache = cache[:, :width]
    value_cache = cache[:, width:]
    row_pos = jnp.take(positions, source, axis=0)
    key_cache = jnp.where(valid[:, None], rotate(key_cache, row_pos), zero)
    return (key_cache, value_cache)


def norm_kernel(x_hbm, gain_hbm, out_ref, lo_ref, hi_ref, x_ref, gain_ref, sem):
    step = 16
    first = lo_ref.shape[0]
    rows = x_ref.shape[0]
    gain_copy = pltpu.make_async_copy(gain_hbm, gain_ref, sem.at[0])
    copies = [
        pltpu.make_async_copy(x_hbm.at[pl.ds(at, step)], x_ref.at[pl.ds(at, step)], sem.at[1 + at // step])
        for at in range(0, rows, step)
    ]
    for copy in copies:
        copy.start()
    gain_copy.start()
    gain_copy.wait()
    gain = gain_ref[...].astype(F32)
    for at, copy in zip(range(0, rows, step), copies):
        copy.wait()
        x = x_ref[at : at + step, :].astype(F32)
        x = x * lax.rsqrt(jnp.mean(x * x, axis=1, keepdims=True) + 1e-06)
        y = [x[:, i * HD : (i + 1) * HD] * gain[i : i + 1, :] for i in range(gain.shape[0])]
        y = jnp.concatenate(y, axis=1).astype(BF)
        out_ref[at : at + step, :] = y
        if at < first:
            lo_ref[at : at + step, :] = y
        else:
            hi_ref[at - first : at - first + step, :] = y


def normalise(hidden, gain):
    rows, wide = hidden.shape
    hbm = pl.BlockSpec(memory_space=ANY)
    return pl.pallas_call(
        norm_kernel,
        out_shape=(VMEM((rows, wide), BF), VMEM((PART[0], wide), BF), pltpu.HBM((PART[1], wide), BF)),
        in_specs=[hbm, hbm],
        scratch_shapes=[
            VMEM((rows, wide), BF),
            VMEM((wide // HD, HD), BF),
            pltpu.SemaphoreType.DMA((1 + rows // 16,)),
        ],
        name="norm",
        cost_estimate=pl.CostEstimate(flops=rows * wide, bytes_accessed=rows, transcendentals=rows),
        compiler_params=pltpu.CompilerParams(vmem_limit_bytes=16 * MIB),
    )(in_hbm(hidden), in_hbm(gain.reshape(wide // HD, HD)))


PART = (32, 32)
PART_AT = (0, 64)


def piece_at(step, part):
    return pl.multiple_of(((lax.axis_index("head") // 2) ^ step) * 128 + PART_AT[part], 32)


def rotation(pieces, cos, sin):
    return [
        jnp.concatenate([table[pl.ds(piece_at(*piece), 2 * PART[piece[1]]), :] for piece in pieces], axis=0)
        for table in (cos, sin)
    ]


def load_rows(x, pieces, sources, sem, start=True, wait=True):
    core = lax.axis_index("head") % 2
    base = 0
    for i, ((step, part), (own, sib, row)) in enumerate(zip(pieces, sources)):
        n = PART[part]
        for j, src in enumerate((own, sib)):
            at = pl.multiple_of(base + (core ^ j) * n, 16)
            copy = pltpu.make_async_copy(src.at[pl.ds(row, n)], x.at[pl.ds(at, n)], sem.at[2 * i + j])
            if start:
                copy.start()
            if wait:
                copy.wait()
        base += 2 * n


def turn(raw, c, s):
    raw = raw.astype(BF).astype(F32)
    heads = []
    for h in range(raw.shape[1] // HD):
        one = raw[:, h * HD : (h + 1) * HD]
        heads.append(one * c + pltpu.roll(one, HD // 2, axis=1) * s)
    return jnp.concatenate(heads, axis=1).astype(BF)


WHOLE = [(0, 0), (0, 1)]


def both(own, sib):
    return [(own, sib, 0), (own, sib, PART[0])]


def wave_kernel(pieces, kind, mode, count, *refs):
    sources = refs[:count]
    wk, wv, kb, vb, cos, sin = refs[count : count + 6]
    outs = refs[count + 6 :]
    if mode == "use":
        x, sem = outs[-2:]
        outs = outs[:-2]
        kept = (wk, wv)
    else:
        x, sem, wsem, blocks = outs[-4:]
        outs = outs[:-4]
    deep, width = wk.shape
    tile = 256
    each = width // tile
    total = 2 * each
    half = deep // 2

    def block(i):
        if mode == "stream":
            return blocks.at[i % blocks.shape[0]]
        return kept[i // each].at[:, pl.ds(i % each * tile, tile)]

    copies = []
    if mode == "stream":
        for i in range(total):
            cols = pl.ds(i % each * tile, tile)
            copies.append(
                [
                    pltpu.make_async_copy(
                        (wk, wv)[i // each].at[pl.ds(j * half, half), cols],
                        block(i).at[pl.ds(j * half, half)],
                        wsem.at[2 * i + j],
                    )
                    for j in range(2)
                ]
            )

    def fetch(i):
        for copy in copies[i]:
            copy.start()

    load = functools.partial(load_rows, x, pieces)
    if kind == "relayed":
        chip = lax.axis_index("head") // 2
        at_end = (chip == 0) | (chip == 3)
        rows = both(*sources[:2])
        ends = both(*sources[2:])
        pl.when(jnp.logical_not(at_end))(lambda: load(rows, sem, wait=False))
        pl.when(at_end)(lambda: load(ends, sem, wait=False))
    else:
        rows = both(*sources) if kind == "whole" else [(sources[i], sources[i + 1], 0) for i in range(0, count, 2)]
        load(rows, sem, wait=False)
    if mode == "stream":
        for i in range(DEPTH):
            fetch(i)
    c, s = rotation(pieces, cos, sin)
    load(rows, sem, start=False)
    part = x.shape[0] // len(outs)
    for i in range(total):
        if copies:
            for copy in copies[i]:
                copy.wait()
        raw = jnp.dot(x[...], block(i)[...], preferred_element_type=F32)
        if i < each:
            y = turn(raw + kb[:, i * tile : (i + 1) * tile].astype(F32), c, s)
        else:
            at = (i - each) * tile
            y = (raw + vb[:, at : at + tile].astype(F32)).astype(BF)
        for k, out in enumerate(outs):
            out[:, i * tile : (i + 1) * tile] = y[k * part : (k + 1) * part]
        if mode == "stream" and i + DEPTH < total:
            fetch(i + DEPTH)


DEPTH = 3


def cost(m, deep, width, weights):
    return pl.CostEstimate(flops=m * width, bytes_accessed=2 * m * width, transcendentals=0)


def in_hbm(x):
    return pltpu.with_memory_space_constraint(x, pltpu.HBM)


def wave(name, pieces, kind, sources, wk, wv, rest, split=1, mode="stream"):
    deep, width = wk.shape
    m = sum(2 * PART[part] for _, part in pieces)
    tile = 256
    full = pl.BlockSpec(memory_space=VMEM)
    hbm = pl.BlockSpec(memory_space=ANY)
    scratch = [VMEM((m, deep), BF), pltpu.SemaphoreType.DMA((2 * len(pieces),))]
    outs = [VMEM((m // split, 2 * width), BF)] * split
    if mode == "stream":
        scratch.append(pltpu.SemaphoreType.DMA((4 * width // tile,)))
        scratch.append(VMEM((DEPTH, deep, tile), BF))
    return pl.pallas_call(
        functools.partial(wave_kernel, pieces, kind, mode, len(sources)),
        out_shape=outs,
        in_specs=[hbm] * len(sources) + [full if mode == "use" else hbm] * 2 + [full] * 4,
        out_specs=[full] * len(outs),
        scratch_shapes=scratch,
        name=name,
        cost_estimate=cost(m, deep, width, True),
        compiler_params=pltpu.CompilerParams(vmem_limit_bytes=(18 if mode == "stream" else 6) * MIB),
    )(*sources, wk, wv, *rest)


def place_kernel(units, own, lengths, owner, *refs):
    count = max(unit[3] for unit in units) + 1
    sources = refs[:count]
    key_out, value_out, rows, cache, held, sem, out_sem = refs[count:]
    width = key_out.shape[1]
    group = lax.axis_index("group")
    chip = lax.axis_index("head") // 2
    copies = []

    def target(d, step, at, n):
        to = pl.multiple_of((group ^ d) * 512 + (chip ^ step) * 128 + at, 16)
        return rows.at[pl.ds(to, n)]

    for d, step, at, a, row, n in units:
        if a in own:
            copies.append(
                pltpu.make_async_copy(sources[a].at[pl.ds(row, n)], target(d, step, at, n), sem.at[len(copies)])
            )
            copies[-1].start()
    for d, step, at, a, row, n in units:
        if a not in own:
            target(d, step, at, n)[...] = sources[a][row : row + n, :]

    def request(q, carry):
        start, local, mine = carry
        length = lengths[q]
        hit = owner[q] == group

        @pl.when(hit)
        def _():
            held[0, mine] = start
            held[1, mine] = local
            held[2, mine] = length

        return (start + length, local + jnp.where(hit, length, 0), mine + jnp.where(hit, 1, 0))

    zero = jnp.int32(0)
    _, _, requests = lax.fori_loop(0, lengths.shape[0], request, (zero, zero, zero))
    for copy in copies:
        copy.wait()
    tile, window = 128, 256
    total = rows.shape[0]
    tiles = cache.shape[0] // tile

    def writes(t):
        top = pl.multiple_of(t * tile, tile)
        return [
            pltpu.make_async_copy(
                cache.at[pl.ds(top, tile), pl.ds(part * width, width)], out.at[pl.ds(top, tile)], out_sem.at[t, part]
            )
            for part, out in enumerate((key_out, value_out))
        ]

    def fill(t, carry):
        top = pl.multiple_of(t * tile, tile)
        cache[pl.ds(top, tile), :] = jnp.zeros((tile, cache.shape[1]), BF)

        def add(q, c):
            start, local, length = held[0, q], held[1, q], held[2, q]

            @pl.when((local < top + tile) & (local + length > top))
            def _():
                base = start + top - local
                at = pl.multiple_of(jnp.clip((base >> 7) << 7, 0, total - window), 128)
                lane = lax.broadcasted_iota(jnp.int32, (tile, window), 1)
                p = lane & 127
                first, second = PART
                stay = (p < first) | (p >= 128 - second)
                src = at + lane + jnp.where(stay, 0, jnp.where(p < 2 * first, second, -first))
                dst = base + lax.broadcasted_iota(jnp.int32, (tile, window), 0)
                hit = (src == dst) & (src >= start) & (src < start + length)
                pick = jnp.where(hit, 1.0, 0.0).astype(BF)
                for i in range(2):
                    cols = slice(i * width, (i + 1) * width)
                    moved = jnp.dot(pick, rows[pl.ds(at, window), cols], preferred_element_type=F32)
                    cache[pl.ds(top, tile), cols] += moved.astype(BF)

            return c

        lax.fori_loop(0, requests, add, 0)
        for write in writes(t):
            write.start()
        return carry

    lax.fori_loop(0, tiles, fill, 0)

    def finish(t, carry):
        for write in writes(t):
            write.wait()
        return carry

    lax.fori_loop(0, tiles, finish, 0)


def place(units, own, arrays, lengths, owner, cap, width, total):
    out = jax.ShapeDtypeStruct((cap, width), BF)
    smem = pl.BlockSpec(memory_space=pltpu.SMEM)
    full = pl.BlockSpec(memory_space=VMEM)
    hbm = pl.BlockSpec(memory_space=ANY)
    return pl.pallas_call(
        functools.partial(place_kernel, units, own),
        out_shape=(out, out),
        in_specs=[smem, smem] + [hbm if i in own else full for i in range(len(arrays))],
        out_specs=(hbm, hbm),
        scratch_shapes=[
            VMEM((total, 2 * width), BF),
            VMEM((cap, 2 * width), BF),
            pltpu.SMEM((3, lengths.shape[0]), jnp.int32),
            pltpu.SemaphoreType.DMA((sum(unit[3] in own for unit in units),)),
            pltpu.SemaphoreType.DMA((cap // 128, 2)),
        ],
        name="place",
        cost_estimate=pl.CostEstimate(flops=0, bytes_accessed=20 * MIB, transcendentals=0),
        compiler_params=pltpu.CompilerParams(vmem_limit_bytes=24 * MIB),
    )(lengths, owner, *arrays)


def pipelined(hidden, norm_gain, k_weight, k_bias, v_weight, v_bias, positions, lengths, owner):
    width = k_weight.shape[1]
    group = lax.axis_index("group")

    def line(x, pairs):
        return lax.ppermute(x, "head", [(2 * a + c, 2 * b + c) for a, b in pairs for c in range(2)])

    def sibling(x):
        return lax.ppermute(x, "head", [(i, i ^ 1) for i in range(8)])

    def across(x, bit):
        return lax.ppermute(x, "group", [(i, i ^ bit) for i in range(4)])

    far_pairs = [(0, 2), (1, 3), (2, 0), (3, 1)]
    near_pairs = [(0, 1), (1, 0), (2, 3), (3, 2)]
    middle_pairs = [(1, 2), (2, 1)]

    def after(x, *done):
        return lax.optimization_barrier((x,) + done)[0]

    own, lo, hi = normalise(hidden, norm_gain)
    own_s = sibling(own)
    far1, near1 = line(lo, far_pairs), line(lo, near_pairs)

    half = HD // 2
    freq = jnp.exp(jnp.arange(half, dtype=F32) * (-2.0 / HD * jnp.log(F32(1000000.0))))
    pos = lax.dynamic_slice(positions, (group * 512,), (512,)).astype(F32)
    pos = pos.reshape(4, 2, 64)
    pos = jnp.concatenate([pos[:, :, : PART[0]].reshape(4, -1), pos[:, :, PART[0] :].reshape(4, -1)], axis=1).reshape(512)
    angle = pos[:, None] * freq[None, :]
    cosine, sine = jnp.cos(angle), jnp.sin(angle)
    cos = jnp.concatenate([cosine, cosine], axis=1)
    sin = jnp.concatenate([-sine, sine], axis=1)
    rest = (k_bias.reshape(1, width), v_bias.reshape(1, width), cos, sin)

    wk, wv = in_hbm(k_weight), in_hbm(v_weight)
    kk, kv = (pltpu.with_memory_space_constraint(w, VMEM) for w in (k_weight, v_weight))
    together = lax.optimization_barrier
    (p0,) = wave("wave0", WHOLE, "whole", [own, own_s], wk, wv, rest)
    far1, near1, p0, lo, hi, own = together((far1, near1, p0, lo, hi, own))

    far2, near2 = line(hi, far_pairs), line(hi, near_pairs)
    x0, y0 = across(p0, 1), across(p0, 2)
    pieces1 = [(2, 0), (1, 0)]
    (p1,) = wave("wave1", pieces1, "pieces", [far1, sibling(far1), near1, sibling(near1)], kk, kv, rest, 1, "use")
    p1, x0, y0 = together((p1, x0, y0))
    x1, y1 = across(p1, 1), across(p1, 2)
    x0, x1, y1, far1, far2, near2, p1, own = together((x0, x1, y1, far1, far2, near2, p1, own))

    middle, relay = line(own, middle_pairs), line(jnp.concatenate([far1, far2]), near_pairs)
    d0, d1 = across(x0, 2), across(y1, 1)
    pieces2 = [(2, 1), (1, 1)]
    p2 = wave("wave2", pieces2, "pieces", [far2, sibling(far2), near2, sibling(near2)], kk, kv, rest, 2, "use")
    d0, d1, *p2 = together((d0, d1, *p2))
    x2, y2 = [across(p, 1) for p in p2], [across(p, 2) for p in p2]
    x2, y2, middle, relay = together((x2, y2, middle, relay))

    d2 = [across(x2[0], 2), across(y2[1], 1)]
    sources = [middle, sibling(middle), relay, sibling(relay)]
    pieces3 = [(3, 0), (3, 1)]
    p3 = wave("wave3", pieces3, "relayed", sources, kk, kv, rest, 2, "use")
    p3, d2 = together((p3, d2))
    x3, y3 = [across(p, 1) for p in p3], [across(p, 2) for p in p3]
    d3 = [across(x3[0], 2), across(y3[1], 1)]

    units, arrays, mine = [], [], set()

    def arrived(pieces, split, got, early=False):
        total = sum(2 * PART[part] for _, part in pieces)
        each = total // split
        for d, parts in enumerate(got):
            row = 0
            if early and d in (1, 2):
                mine.add(len(arrays) + split - 1)
                parts = [*parts[:-1], in_hbm(parts[-1])]
            for step, part in pieces:
                done = 0
                while done < 2 * PART[part]:
                    i = (row + done) // each
                    n = min(2 * PART[part] - done, (i + 1) * each - row - done)
                    units.append((d, step, PART_AT[part] + done, len(arrays) + i, row + done - i * each, n))
                    done += n
                row += done
            arrays.extend(parts)

    arrived(WHOLE, 1, [[one] for one in (p0, x0, y0, d0)])
    arrived(pieces1, 1, [[one] for one in (p1, x1, y1, d1)])
    arrived(pieces2, 2, (p2, x2, y2, d2), True)
    arrived(pieces3, 2, (p3, x3, y3, d3))
    return place(units, sorted(mine), arrays, lengths, owner, 1024, width, 2048)


def solution(mesh):
    in_specs = (
        P(("group", "head"), None),
        P(),
        P(None, "head"),
        P("head"),
        P(None, "head"),
        P("head"),
        P(),
        P(),
        P(),
    )
    out_specs = (P("group", "head"), P("group", "head"))
    square = mesh.shape["group"] == 4 and mesh.shape["head"] == 8
    return jax.shard_map(
        pipelined if square else gathered, mesh=mesh, in_specs=in_specs, out_specs=out_specs, check_vma=False
    )
```
